512 devices in a mesh: leaf: 8 (over x, core), bulk: 64 (over y, z).
Axes of the slice: x: 4, y: 4, z: 16, core: 2. Of those that a mesh axis runs over, the one named last changes fastest.
Arguments:
- particles: float32 [16384, 4, 512], P(('leaf', 'bulk')), may hold values from -6 to 6
- velocities: float32 [16384, 3, 512], P(('leaf', 'bulk')), may hold values from -6 to 6
- cell_table: float32 [10, 131072], P(None, ('leaf', 'bulk')), may hold values from -8 to 8
- top_cells: float32 [10, 512], P(None, 'leaf'), may hold values from -12 to 12
- active_ids: int32 [2048], P(('leaf', 'bulk')), may hold values from 0 to 31, as said below
- active_count: int32 [512], P(('leaf', 'bulk')), may hold values from 1 to 4, as said below
- cell_requests: int32 [512, 64, 16], P(('leaf', 'bulk')), may hold values from -1 to 255, as said below
- cell_lists: int32 [2048, 64], P(('leaf', 'bulk')), may hold values from 0 to 1023, as said below
- leaf_requests: int32 [512, 64, 2], P(('leaf', 'bulk')), may hold values from -1 to 31, as said below
- leaf_lists: int32 [2048, 6], P(('leaf', 'bulk')), may hold values from 0 to 127, as said below
- targets: int32 [16384], P(('leaf', 'bulk')), may hold values from 0 to 63, as said below
Outputs:
- moved_particles: float32 [16384, 4, 512], P(('leaf', 'bulk'))
- moved_velocities: float32 [16384, 3, 512], P(('leaf', 'bulk'))
The draws below stay inside these ranges and needn't reach their ends.
Inputs may be any that keep to these rules, and one draw needn't show every extreme that they name: `active_ids`: one device's 4 entries are distinct buckets of that device; only its first active_count entries are active. `active_count`: some device has 4 in every draw. `cell_requests`: entry [r, p, k] names a cell of bulk index p of r's leaf group, or is -1 for an unused slot; in each row [r, p] the used entries come first, are distinct and number 8 or more; in every draw one bulk index of each leaf group receives 16 from every device of it. `cell_lists`: entry f names slot f mod 16 of bulk peer f // 16 in its device's row of cell_requests, always a used one; one slot's entries are distinct. `leaf_requests`: entry [r, p, k] names a bucket of bulk index p of r's leaf group, or is -1 for an unused slot; no device asks its own bulk index; for every other peer the used entries come first, are distinct and number 1 or more; in every draw one bulk index of each leaf group receives 2 from every other device of it. `leaf_lists`: entry f names slot f mod 2 of bulk peer f // 2 in its device's row of leaf_requests, always a used one; one slot's entries are distinct. `targets`: within one leaf group, bucket j of the device with bulk index s goes to bulk index (s + t) mod 64, where the shift t depends only on the group and j; each device sends exactly 2 buckets to each of 16 bulk indices; the shifts 1 and 32 are among those of every group.
All inputs are finite; a program needn't handle non-finite values.
Results may differ from the reference program's by a relative error of at most 0.0003.
Values sent between devices are 32-bit elements; how exact they have to be, the bound alone decides.
A program may use at most 64 MiB of HBM per device.

```python
import math
import jax
import jax.numpy as jnp
from jax import lax

B = 512
BUCK_DEV = 32
CELL_DEV = 256
TOP_DEV = 64
ACT_MAX = 4
CELLS_PER = 64
LEAVES_PER = 6
CCAP = 16
LCAP = 2
PEERS = 64
DOMAINS = 8
RANKS = 512
MOST = 2
BUCKETS = 16384
CELLS = 131072
TOP = 512
SLOTS = 2048


def stack_moments(key, count, mass_scale, centre, tensor_unit):
    masses = mass_scale * jnp.exp(jax.random.uniform(key, (1, count), jnp.float32, math.log(0.5), math.log(2.0)))
    return jnp.concatenate([masses, centre, tensor_unit * masses], axis=0)


def draw_particles(key, part):
    key = jax.random.fold_in(key, 1)
    key_place, key_mass = jax.random.split(key)
    places = jnp.clip(jax.random.normal(key_place, (BUCKETS, 3, B), jnp.float32), -6.0, 6.0)
    masses = jnp.exp(jax.random.uniform(key_mass, (BUCKETS, 1, B), jnp.float32, math.log(0.5), math.log(2.0)))
    return jnp.concatenate([places, masses], axis=1)


def draw_cell_table(key, part):
    key = jax.random.fold_in(key, 2)
    key_mass, key_centre, key_tensor = jax.random.split(key, 3)
    centre = jnp.clip(2.0 * jax.random.normal(key_centre, (3, CELLS), jnp.float32), -8.0, 8.0)
    tensor_unit = jnp.clip(0.5 * jax.random.normal(key_tensor, (6, CELLS), jnp.float32), -2.0, 2.0)
    return stack_moments(key_mass, CELLS, 1.0 / CELLS_PER, centre, tensor_unit)


def draw_top_cells(key, part):
    key = jax.random.fold_in(key, 3)
    key_mass, key_centre, key_tensor = jax.random.split(key, 3)
    centre = jnp.clip(3.0 * jax.random.normal(key_centre, (3, TOP), jnp.float32), -12.0, 12.0)
    tensor_unit = jnp.clip(0.5 * jax.random.normal(key_tensor, (6, TOP), jnp.float32), -2.0, 2.0)
    return stack_moments(key_mass, TOP, 4.0 / TOP_DEV, centre, tensor_unit)


def active_layout(key):
    key_order, key_pair, key_hot = jax.random.split(key, 3)
    scores = jax.random.randint(key_order, (RANKS, BUCK_DEV), 0, 1 << 16) * BUCK_DEV + jnp.arange(BUCK_DEV, dtype=jnp.int32)[None, :]
    chosen = jnp.argsort(scores, axis=1)[:, :ACT_MAX].astype(jnp.int32)
    pair_draw = jax.random.randint(key_pair, (2, RANKS), 0, ACT_MAX)
    counts = 1 + jnp.minimum(pair_draw[0], pair_draw[1])
    hot_rank = jax.random.randint(key_hot, (), 0, RANKS)
    counts = jnp.where(jnp.arange(RANKS, dtype=jnp.int32) == hot_rank, ACT_MAX, counts)
    return (chosen.reshape(-1), counts.astype(jnp.int32))


def draw_active_ids(key, part):
    chosen, counts = active_layout(jax.random.fold_in(key, 100))
    return chosen


def draw_active_count(key, part):
    chosen, counts = active_layout(jax.random.fold_in(key, 100))
    return counts


def request_layout(key, cap, pool, list_len, skip_self):
    key_list = jax.random.split(key, 5)
    counts = jax.random.randint(key_list[0], (RANKS, PEERS), cap // 2, cap + 1)
    hot_owner = jax.random.randint(key_list[1], (DOMAINS,), 0, PEERS)
    rank_ids = jnp.arange(RANKS, dtype=jnp.int32)
    peer_ids = jnp.arange(PEERS, dtype=jnp.int32)
    counts = jnp.where(peer_ids[None, :] == hot_owner[rank_ids // PEERS][:, None], cap, counts)
    if skip_self:
        counts = jnp.where(peer_ids[None, :] == (rank_ids % PEERS)[:, None], 0, counts)
    start_at = jax.random.randint(key_list[2], (RANKS, PEERS, 1), 0, pool)
    stride = 2 * jax.random.randint(key_list[3], (RANKS, PEERS, 1), 0, pool // 2) + 1
    places = jnp.arange(cap, dtype=jnp.int32)[None, None, :]
    entries = (start_at + places * stride) % pool
    used_mask = places < counts[:, :, None]
    requests = jnp.where(used_mask, entries, -1)
    width_all = PEERS * cap
    flat_used = used_mask.reshape(RANKS, width_all)
    position = jnp.arange(width_all, dtype=jnp.int32)[None, :]
    scores = jax.random.randint(key_list[4], (RANKS, width_all), 0, 1 << 16) * width_all + position
    scores = jnp.where(flat_used, scores, (1 << 30) + position)
    order_ids = jnp.argsort(scores, axis=1)
    total_used = jnp.sum(counts, axis=1)
    walk_ids = jnp.arange(ACT_MAX * list_len, dtype=jnp.int32)[None, :] % total_used[:, None]
    list_ids = jnp.take_along_axis(order_ids, walk_ids, axis=1).reshape(RANKS * ACT_MAX, list_len)
    return (requests.astype(jnp.int32), list_ids.astype(jnp.int32))


def draw_cell_requests(key, part):
    requests, list_ids = request_layout(jax.random.fold_in(key, 200), CCAP, CELL_DEV, CELLS_PER, False)
    return requests


def draw_cell_lists(key, part):
    requests, list_ids = request_layout(jax.random.fold_in(key, 200), CCAP, CELL_DEV, CELLS_PER, False)
    return list_ids


def draw_leaf_requests(key, part):
    requests, list_ids = request_layout(jax.random.fold_in(key, 300), LCAP, BUCK_DEV, LEAVES_PER, True)
    return requests


def draw_leaf_lists(key, part):
    requests, list_ids = request_layout(jax.random.fold_in(key, 300), LCAP, BUCK_DEV, LEAVES_PER, True)
    return list_ids


def draw_targets(key, part):
    key = jax.random.fold_in(key, 4)
    key_value, key_assign = jax.random.split(key)
    peer_ids = jnp.arange(PEERS, dtype=jnp.int32)[None, :]
    forced = (peer_ids == 1) | (peer_ids == PEERS // 2)
    value_scores = (jax.random.randint(key_value, (DOMAINS, PEERS), 0, 1 << 16) + 1) * PEERS + peer_ids
    value_scores = jnp.where(forced, peer_ids, value_scores)
    shift_values = jnp.argsort(value_scores, axis=1)[:, :BUCK_DEV // MOST].astype(jnp.int32)
    assign_scores = jax.random.randint(key_assign, (DOMAINS, BUCK_DEV), 0, 1 << 16) * BUCK_DEV + jnp.arange(BUCK_DEV, dtype=jnp.int32)[None, :]
    places = jnp.argsort(jnp.argsort(assign_scores, axis=1), axis=1)
    shifts = jnp.take_along_axis(shift_values, places // MOST, axis=1)
    bulk_ids = jnp.arange(PEERS, dtype=jnp.int32)[None, :, None]
    result = (bulk_ids + shifts[:, None, :]) % PEERS
    return result.reshape(-1).astype(jnp.int32)


def block_scale(stream_key, extent, cuts, low, high):
    loudness = 1.0
    for axis_at, shards_of in cuts:
        heights = jax.random.uniform(jax.random.fold_in(jax.random.fold_in(stream_key, 6), axis_at), (shards_of,), jnp.float32, low / len(cuts), high / len(cuts))
        loudness = loudness * jnp.repeat(jnp.exp(heights), extent[axis_at] // shards_of).reshape((-1,) + (1,) * (len(extent) - 1 - axis_at))
    return loudness


def gaussian(rng, extent, deviation, most, shards=(), kind=jnp.bfloat16):
    array = deviation * jax.random.normal(rng, extent, jnp.float32)
    if shards:
        array = array * block_scale(rng, extent, shards, -0.22, 0.18)
    return jnp.clip(array, -most, most).astype(kind)


def setup_inputs(seed: int = 0) -> dict:
    streams_of = jax.random.split(jax.random.key(seed), 12)
    particles = draw_particles(jax.random.fold_in(streams_of[11], 71), 0)
    velocities = gaussian(streams_of[1], (BUCKETS, 3, B), 1.0, 6.0, ((0, 512),), jnp.float32)
    cell_table = draw_cell_table(jax.random.fold_in(streams_of[11], 71), 0)
    top_cells = draw_top_cells(jax.random.fold_in(streams_of[11], 71), 0)
    active_ids = draw_active_ids(jax.random.fold_in(streams_of[11], 71), 0)
    active_count = draw_active_count(jax.random.fold_in(streams_of[11], 71), 0)
    cell_requests = draw_cell_requests(jax.random.fold_in(streams_of[11], 71), 0)
    cell_lists = draw_cell_lists(jax.random.fold_in(streams_of[11], 71), 0)
    leaf_requests = draw_leaf_requests(jax.random.fold_in(streams_of[11], 71), 0)
    leaf_lists = draw_leaf_lists(jax.random.fold_in(streams_of[11], 71), 0)
    targets = draw_targets(jax.random.fold_in(streams_of[11], 71), 0)
    return {"particles": particles, "velocities": velocities, "cell_table": cell_table, "top_cells": top_cells, "active_ids": active_ids, "active_count": active_count, "cell_requests": cell_requests, "cell_lists": cell_lists, "leaf_requests": leaf_requests, "leaf_lists": leaf_lists, "targets": targets}


step_time = 0.5
pair_soft = 0.01
cell_soft = 1.0

def cell_pull(points, moments):
    sep_x = points[0][:, None] - moments[1][None, :]
    sep_y = points[1][:, None] - moments[2][None, :]
    sep_z = points[2][:, None] - moments[3][None, :]
    inv_one = lax.rsqrt(sep_x * sep_x + sep_y * sep_y + sep_z * sep_z + cell_soft)
    inv_two = inv_one * inv_one
    inv_three = inv_two * inv_one
    inv_five = inv_three * inv_two
    tensor_x = moments[4] * sep_x + moments[7] * sep_y + moments[8] * sep_z
    tensor_y = moments[7] * sep_x + moments[5] * sep_y + moments[9] * sep_z
    tensor_z = moments[8] * sep_x + moments[9] * sep_y + moments[6] * sep_z
    quadric = sep_x * tensor_x + sep_y * tensor_y + sep_z * tensor_z
    radial = -moments[0] * inv_three - 2.5 * quadric * inv_five * inv_two
    pull_x = lax.optimization_barrier(jnp.sum(radial * sep_x + tensor_x * inv_five, axis=1))
    pull_y = lax.optimization_barrier(jnp.sum(radial * sep_y + tensor_y * inv_five, axis=1))
    pull_z = lax.optimization_barrier(jnp.sum(radial * sep_z + tensor_z * inv_five, axis=1))
    return jnp.stack([pull_x, pull_y, pull_z])

def pair_pull(points, sources):
    pair_scale = 1.0 / sources.shape[1]
    sep_x = sources[0][None, :] - points[0][:, None]
    sep_y = sources[1][None, :] - points[1][:, None]
    sep_z = sources[2][None, :] - points[2][:, None]
    inv_one = lax.rsqrt(sep_x * sep_x + sep_y * sep_y + sep_z * sep_z + pair_soft)
    weighted = (sources[3] * pair_scale)[None, :] * inv_one * inv_one * inv_one
    return jnp.stack([lax.optimization_barrier(jnp.sum(weighted * sep_x, axis=1)), lax.optimization_barrier(jnp.sum(weighted * sep_y, axis=1)), lax.optimization_barrier(jnp.sum(weighted * sep_z, axis=1))])

def reference(particles, velocities, cell_table, top_cells, active_ids, active_count, cell_requests, cell_lists, leaf_requests, leaf_lists, targets):
    slot_ids = jnp.arange(SLOTS, dtype=jnp.int32)

    def one_slot(slot_id):
        rank_id = slot_id // ACT_MAX
        group_first = rank_id // PEERS * PEERS
        bucket = rank_id * BUCK_DEV + active_ids[slot_id]
        own_bucket = particles[bucket]
        cell_picks = cell_lists[slot_id]
        owners = cell_picks // CCAP
        columns = (group_first + owners) * CELL_DEV + cell_requests[rank_id, owners, cell_picks % CCAP]
        chosen = cell_table[:, columns]
        leaf_picks = leaf_lists[slot_id]
        leaf_owners = leaf_picks // LCAP
        leaf_ids = (group_first + leaf_owners) * BUCK_DEV + leaf_requests[rank_id, leaf_owners, leaf_picks % LCAP]
        sources = jnp.concatenate([own_bucket[None], particles[leaf_ids]], axis=0)
        flat_sources = jnp.transpose(sources, (1, 0, 2)).reshape(4, -1)
        points = own_bucket[:3]
        return cell_pull(points, chosen) + cell_pull(points, top_cells) + pair_pull(points, flat_sources)
    pulls_total = lax.map(one_slot, slot_ids)
    alive_mask = (jnp.arange(ACT_MAX, dtype=jnp.int32)[None, :] < active_count[:, None]).reshape(-1).astype(jnp.float32)
    kick_terms = step_time * pulls_total * alive_mask[:, None, None]
    bucket_ids = slot_ids // ACT_MAX * BUCK_DEV + active_ids
    new_speed = velocities.at[bucket_ids].add(kick_terms)
    new_place = particles[:, :3] + step_time * new_speed
    new_state = jnp.concatenate([new_place, particles[:, 3:]], axis=1)
    bucket_all = jnp.arange(BUCKETS, dtype=jnp.int32)
    destination = (bucket_all // BUCK_DEV // PEERS * PEERS + targets) * BUCK_DEV + bucket_all % BUCK_DEV
    moved_particles = jnp.zeros_like(new_state).at[destination].set(new_state)
    moved_velocities = jnp.zeros_like(new_speed).at[destination].set(new_speed)
    return (moved_particles, moved_velocities)
```

```python
import functools

import jax
import jax.numpy as jnp
from jax import lax
from jax.experimental import pallas as pl
from jax.experimental.pallas import tpu as pltpu
from jax.sharding import PartitionSpec as P

MESH = pl.DeviceIdType.MESH
step_time = 0.5
pair_soft = 0.01
cell_soft = 1.0

NY, NZ, NL = 4, 16, 8
NB = 32
ACT = 4
LPER = 6
CPER = 64
SUBS = 4
SROW = NB // SUBS
OCT = 64


def pair_terms(px, py, pz, src, accs):
    ax, ay, az = accs
    for sx, sy, sz, sm in src:
        dx = sx - px
        dy = sy - py
        dz = sz - pz
        inv = lax.rsqrt(dx * dx + dy * dy + (dz * dz + pair_soft))
        w = sm * inv * (inv * inv)
        ax = ax + w * dx
        ay = ay + w * dy
        az = az + w * dz
    return ax, ay, az


def cell_terms(px, py, pz, cells, accs):
    ax, ay, az = accs
    for m, cx, cy, cz, xx, yy, zz, xy, xz, yz in cells:
        dx = px - cx
        dy = py - cy
        dz = pz - cz
        inv = lax.rsqrt(dx * dx + dy * dy + (dz * dz + cell_soft))
        inv2 = inv * inv
        inv3 = inv2 * inv
        inv5 = inv3 * inv2
        tx = xx * dx + xy * dy + xz * dz
        ty = xy * dx + yy * dy + yz * dz
        tz = xz * dx + yz * dy + zz * dz
        u = dx * tx + dy * ty + dz * tz
        rad = m * inv3 + (2.5 * u) * (inv5 * inv2)
        ax = ax + (tx * inv5 - rad * dx)
        ay = ay + (ty * inv5 - rad * dy)
        az = az + (tz * inv5 - rad * dz)
    return ax, ay, az


def kernel(
    part, vel, cells, top, act_ids, act_cnt, cell_lists, cell_req, leaf_req, leaf_lists, targets,
    outp, outv,
    p_all, v_all, v_y, c_all, t_all, top_m, codes_v, codes_s, l_send,
    l0, l1, l2, l3, k0, k1, k2, k3, p_rec, pts, acc, own, chosen, picks, near,
    p_ss, p_rs, c_ss, c_rs, v_ss, v_rs, t_ss, t_rs, d_ss, d_rs, vy_ss, vy_rs,
    cy_ss, cy_rs, l_ss, l_rs, pr_ss, pr_rs, kz_ss, kz_rs, ky_ss, ky_rs, loc,
):
    l_rec = (l0, l1, l2, l3)
    k_all = (k0, k1, k2, k3)
    leaf = lax.axis_index("leaf")
    bulk = lax.axis_index("bulk")
    y = bulk // NZ
    z = bulk % NZ

    def row_peer(d):
        return y * NZ + (z + d) % NZ

    def col_peer(d):
        return ((y + d) % NY) * NZ + z

    own_p = pltpu.make_async_copy(part, p_all.at[z], loc.at[0])
    own_v = pltpu.make_async_copy(vel, v_y.at[y], loc.at[1])
    own_c = pltpu.make_async_copy(cells, c_all.at[bulk], loc.at[2])
    own_t = pltpu.make_async_copy(top, t_all.at[leaf], loc.at[3])
    own_p.start()
    own_v.start()
    own_c.start()
    own_t.start()

    def code_of(a, e):
        f = leaf_lists[a, e]
        peer = f // LCAP
        return peer * NB + leaf_req[f % LCAP, peer]

    LCAP = 2
    rows = lax.broadcasted_iota(jnp.int32, (8, 128), 0)
    lanes = lax.broadcasted_iota(jnp.int32, (8, 128), 1)
    code = jnp.zeros((8, 128), jnp.int32)
    for a in range(ACT):
        for e in range(LPER):
            code = jnp.where((rows == a) & (lanes == e), code_of(a, e), code)
    codes_v[y] = code

    barrier = pltpu.get_barrier_semaphore()

    def greet(dev):
        pl.semaphore_signal(barrier, inc=1, device_id=dev, device_id_type=MESH)

    for d in range(1, NZ):
        greet({"bulk": row_peer(d)})
    for d in range(1, NY):
        greet({"bulk": col_peer(d)})
    for d in range(1, NL):
        greet({"leaf": (leaf + d) % NL})
    pl.semaphore_wait(barrier, NZ + NY + NL - 3)

    def remote(src, dst, ss, rs, dev):
        return pltpu.make_async_remote_copy(
            src_ref=src, dst_ref=dst, send_sem=ss, recv_sem=rs, device_id=dev, device_id_type=MESH
        )

    def ring_dev(way):
        return {"bulk": row_peer(1 if way == 0 else NZ - 1)}

    def ring_src(way, h):
        return (z + NZ - h) % NZ if way == 0 else (z + h) % NZ

    def p_copy(way, h, sub, first=False):
        at = ring_src(way, h)
        cut = pl.ds(sub * SROW, SROW)
        dst = p_all.at[at, cut]
        src = part.at[cut] if first else dst
        return remote(src, dst, p_ss.at[way, h, sub], p_rs.at[way, h, sub], ring_dev(way))

    def c_copy(way, h):
        at = c_all.at[y * NZ + ring_src(way, h)]
        src = cells if isinstance(h, int) and h == 0 else at
        return remote(src, at, c_ss.at[way, h], c_rs.at[way, h], ring_dev(way))

    def v_copy(way, h, sub):
        at = v_all.at[ring_src(way, h), sub]
        return remote(at, at, v_ss.at[way, h, sub], v_rs.at[way, h, sub], ring_dev(way))

    def t_copy(d):
        return remote(top, t_all.at[leaf], t_ss.at[d], t_rs.at[d], {"leaf": (leaf + d) % NL})

    def d_copy(d):
        return remote(
            codes_v.at[y], codes_v.at[y], d_ss.at[d], d_rs.at[d], {"bulk": col_peer(d)}
        )

    def vy_copy(d):
        return remote(vel, v_y.at[y], vy_ss.at[d], vy_rs.at[d], {"bulk": col_peer(d)})

    def cy_copy(d):
        blk = c_all.at[pl.ds(y * NZ, NZ)]
        return remote(blk, blk, cy_ss.at[d], cy_rs.at[d], {"bulk": col_peer(d)})

    def l_copy(a, d):
        return remote(
            l_send.at[d - 1, a], l_rec[a].at[y], l_ss.at[a, d], l_rs.at[a, d],
            {"bulk": col_peer(d)},
        )

    def pr_copy(d):
        return remote(
            p_rec.at[y], p_rec.at[y], pr_ss.at[d], pr_rs.at[d], {"bulk": col_peer(d)}
        )

    def kz_copy(a, d):
        at = k_all[a].at[y, z]
        return remote(at, at, kz_ss.at[a, d], kz_rs.at[a, d], {"bulk": row_peer(d)})

    def ky_copy(a, d):
        at = k_all[a].at[y]
        return remote(at, at, ky_ss.at[a, d], ky_rs.at[a, d], {"bulk": col_peer(d)})

    for d in range(1, NL):
        t_copy(d).start()
    for way in range(2):
        c_copy(way, 0).start()
    for d in range(1, NY):
        d_copy(d).start()
    for sub in range(SUBS):
        for way in range(2):
            p_copy(way, 0, sub, True).start()
    for d in range(1, NY):
        vy_copy(d).start()

    for a in range(ACT):
        bucket = part[act_ids[a]]
        own[a, pl.ds(0, 4), :] = bucket

        def spread(c, _, a=a):
            row = own[a, pl.ds(c, 1), :]
            pts[a, c] = jnp.transpose(jnp.broadcast_to(row, (128, 512)))
            return 0

        lax.fori_loop(0, 3, spread, 0)

    own_t.wait()
    for d in range(1, NL):
        t_copy(d).wait_recv()
    half = lax.broadcasted_iota(jnp.int32, (16, 128), 1) < 64
    for i in range(4):
        top_m[:, pl.ds(i * 128, 128)] = jnp.where(
            half, t_all[2 * i], pltpu.roll(t_all[2 * i + 1], 64, 1)
        )

    def src_rows(load, tiles=4):
        out = []
        for i in range(tiles):
            sx, sy, sz, sm = [load(c, pl.ds(i * 128, 128)) for c in range(4)]
            out.append((sx, sy, sz, sm * (1.0 / (512.0 * (LPER + 1)))))
        return out

    def self_top(a, o0, count):
        src = src_rows(lambda c, cut: own[a, pl.ds(c, 1), cut])

        def step(i, _):
            at = pl.ds(pl.multiple_of((o0 + i) * 8, 8), 8)
            px, py, pz = pts[a, 0, at, :], pts[a, 1, at, :], pts[a, 2, at, :]
            zero = jnp.zeros((8, 128), jnp.float32)
            accs = pair_terms(px, py, pz, src, (zero, zero, zero))
            tops = [
                [top_m[pl.ds(k, 1), pl.ds(j * 128, 128)] for k in range(10)] for j in range(4)
            ]
            accs = cell_terms(px, py, pz, tops, accs)
            for c in range(3):
                acc[a, c, at, :] = accs[c]
            return 0

        lax.fori_loop(0, count, step, 0)

    def near_part(a, o0, count):
        cut = pl.ds(pl.multiple_of((a // 2) * 128, 128), 128)
        lane = lax.broadcasted_iota(jnp.int32, (1, 128), 1)
        mine = (lane // CPER) == (a % 2)
        cell = [near[pl.ds(k, 1), cut] for k in range(10)]
        cell = [v if 1 <= k <= 3 else jnp.where(mine, v, 0.0) for k, v in enumerate(cell)]

        def step(i, _):
            at = pl.ds(pl.multiple_of((o0 + i) * 8, 8), 8)
            px, py, pz = pts[a, 0, at, :], pts[a, 1, at, :], pts[a, 2, at, :]
            accs = tuple(acc[a, c, at, :] for c in range(3))
            accs = cell_terms(px, py, pz, [cell], accs)
            for c in range(3):
                acc[a, c, at, :] = accs[c]
            return 0

        lax.fori_loop(0, count, step, 0)

    def p_event(i):
        h = i // SUBS
        sub = i % SUBS
        for way in range(2):
            mine = (sub < SUBS // 2) if way == 0 else (sub >= SUBS // 2)

            @pl.when((h < NZ // 2 - 1) | mine)
            def _():
                p_copy(way, h, sub).wait_recv()

            @pl.when((h < NZ // 2 - 2) | ((h == NZ // 2 - 2) & mine))
            def _():
                p_copy(way, h + 1, sub).start()

    def c_event(i):
        for way in range(2):
            if way == 0:
                c_copy(way, i).wait_recv()

                @pl.when(i < NZ // 2 - 1)
                def _():
                    c_copy(way, i + 1).start()
            else:

                @pl.when(i < NZ // 2 - 1)
                def _():
                    c_copy(way, i).wait_recv()

                @pl.when(i < NZ // 2 - 2)
                def _():
                    c_copy(way, i + 1).start()

    own_c.wait()

    def first_events(i, _):
        c_event(i)
        p_event(i)
        self_top(i // 8, (i % 8) * 8, 8)
        return 0

    lax.fori_loop(0, 8, first_events, 0)
    for d in range(1, NY):
        cy_copy(d).start()

    def more_events(i, _):
        p_event(i)
        self_top(i // 8, (i % 8) * 8, 8)
        return 0

    lax.fori_loop(8, 16, more_events, 0)

    own_v.wait()
    for d in range(1, NY):
        vy_copy(d).wait_recv()

    def pick_row(j, _):
        shift = (targets[j] - bulk) & 63
        to_z = (z + shift) & 15
        from_y = ((y * NZ + to_z - shift) & 63) >> 4
        for c in range(3):
            v_all[z, c, pl.ds(j, 1), :] = v_y[from_y, c, pl.ds(j, 1), :]
        return 0

    lax.fori_loop(0, NB, pick_row, 0)
    lax.fori_loop(16, 24, more_events, 0)

    for d in range(1, NY):
        cy_copy(d).wait_recv()

    def pick_cell(i, _):
        f = cell_lists[i // CPER, i % CPER]
        peer = f >> 4
        col = cell_req[f & 15, peer] & 255
        chosen[pl.ds(i, 1), :] = c_all[peer, pl.ds(col >> 3, 1), :]
        picks[pl.ds(i, 1), :] = jnp.full((1, 128), col & 7, jnp.int32)
        return 0

    lax.fori_loop(0, ACT * CPER, pick_cell, 0)
    got = chosen[...]
    group = picks[...]
    packed = jnp.where(group == 0, got, 0.0)
    for g in range(1, 8):
        packed = jnp.where(group == g, pltpu.roll(got, 128 - 16 * g, 1), packed)
    near[...] = jnp.transpose(packed)

    def last_events(i, _):
        p_event(i)
        self_top(i // 8, (i % 8) * 8, 8)
        return 0

    lax.fori_loop(24, 32, last_events, 0)

    own_p.wait()
    for d in range(1, NY):
        d_copy(d).wait_recv()
    codes_copy = pltpu.make_async_copy(codes_v, codes_s, loc.at[4])
    codes_copy.start()
    codes_copy.wait()

    def leaf_at(number):
        return p_all[(number >> 5) & 15, number & 31]

    for a in range(ACT):
        for d in range(1, NY):
            to_y = (y + d) % NY

            def fill(e, _, a=a, d=d, to_y=to_y):
                l_send[d - 1, a, e] = leaf_at(codes_s[to_y, a, e])
                return 0

            lax.fori_loop(0, LPER, fill, 0)
            l_copy(a, d).start()

        def fill_own(e, _, a=a):
            l_rec[a][y, e] = leaf_at(code_of(a, e))
            return 0

        lax.fori_loop(0, LPER, fill_own, 0)

    for way in range(2):
        for sub in range(3):
            v_copy(way, 0, sub).start()

    def pick_moved(j, _):
        from_z = (bulk - (targets[j] - bulk)) & 15
        p_rec[y, j] = p_all[from_z, j]
        return 0

    lax.fori_loop(0, NB, pick_moved, 0)
    for d in range(1, NY):
        pr_copy(d).start()

    for a in range(ACT):
        near_part(a, 0, OCT)

    def v_event(i):
        h = i // 3
        sub = i % 3
        for way in range(2):
            mine = (sub == 0) if way == 0 else (sub > 0)

            @pl.when((h < NZ // 2 - 1) | mine)
            def _():
                v_copy(way, h, sub).wait_recv()

            @pl.when((h < NZ // 2 - 2) | ((h == NZ // 2 - 2) & mine))
            def _():
                v_copy(way, h + 1, sub).start()

    def y_send(a):
        def wait_one(d, _):
            kz_copy(a, d).wait_recv()
            return 0

        lax.fori_loop(1, NZ, wait_one, 0)
        for d in range(1, NY):
            ky_copy(a, d).start()

    for a in range(ACT):
        for d in range(1, NY):
            l_copy(a, d).wait_recv()

        def block(e, _, a=a):
            from_y = (code_of(a, e) >> 9) & 3
            src = src_rows(lambda c, cut: l_rec[a][from_y, e, pl.ds(c, 1), cut])

            def step(i, _):
                at = pl.ds(pl.multiple_of(i * 8, 8), 8)
                px, py, pz = pts[a, 0, at, :], pts[a, 1, at, :], pts[a, 2, at, :]
                accs = tuple(acc[a, c, at, :] for c in range(3))
                accs = pair_terms(px, py, pz, src, accs)
                for c in range(3):
                    acc[a, c, at, :] = accs[c]
                return 0

            lax.fori_loop(0, OCT, step, 0)

            @pl.when(e % 2 == 1)
            def _():
                v_event(a * 3 + e // 2)

            return 0

        lax.fori_loop(0, LPER, block, 0)
        alive = jnp.where(a < act_cnt[0], 1.0, 0.0)
        ident = jnp.where(a < act_cnt[0], act_ids[a], -1).astype(jnp.float32)
        for c in range(3):
            pull = jnp.sum(jnp.transpose(acc[a, c]), axis=0, keepdims=True)
            k_all[a][y, z, pl.ds(c, 1), :] = step_time * pull * alive
        k_all[a][y, z, pl.ds(3, 1), :] = jnp.full((1, 512), ident, jnp.float32)

        def send_one(d, _, a=a):
            kz_copy(a, d).start()
            return 0

        lax.fori_loop(1, NZ, send_one, 0)
        if a > 0:
            y_send(a - 1)

    def tail_events(i, _):
        v_event(i)
        return 0

    lax.fori_loop(12, 24, tail_events, 0)
    y_send(ACT - 1)
    for d in range(1, NY):
        pr_copy(d).wait_recv()
    for a in range(ACT):
        for d in range(1, NY):
            ky_copy(a, d).wait_recv()

    def place(j, _):
        source = (bulk - (targets[j] - bulk)) & 63
        from_y = source >> 4
        from_z = source & 15
        number = j.astype(jnp.float32)
        hits = [k_all[a][from_y, from_z, pl.ds(3, 1), :] == number for a in range(ACT)]
        for c in range(3):
            speed = v_all[from_z, c, pl.ds(j, 1), :]
            kick = jnp.zeros((1, 512), jnp.float32)
            for a in range(ACT):
                kick = kick + jnp.where(
                    hits[a], k_all[a][from_y, from_z, pl.ds(c, 1), :], 0.0
                )
            speed = speed + kick
            outv[c, pl.ds(j, 1), :] = speed
            outp[j, pl.ds(c, 1), :] = p_rec[from_y, j, pl.ds(c, 1), :] + step_time * speed
        outp[j, pl.ds(3, 1), :] = p_rec[from_y, j, pl.ds(3, 1), :]
        return 0

    lax.fori_loop(0, NB, place, 0)

    for d in range(1, NL):
        t_copy(d).wait_send()

    def p_sent(i, _):
        h = i // SUBS
        sub = i % SUBS
        for way in range(2):
            mine = (sub < SUBS // 2) if way == 0 else (sub >= SUBS // 2)

            @pl.when((h < NZ // 2 - 1) | mine)
            def _():
                p_copy(way, h, sub).wait_send()

        return 0

    lax.fori_loop(0, 32, p_sent, 0)

    def v_sent(i, _):
        h = i // 3
        sub = i % 3
        for way in range(2):
            mine = (sub == 0) if way == 0 else (sub > 0)

            @pl.when((h < NZ // 2 - 1) | mine)
            def _():
                v_copy(way, h, sub).wait_send()

        return 0

    lax.fori_loop(0, 24, v_sent, 0)
    for h in range(NZ // 2):
        c_copy(0, h).wait_send()
        if h < NZ // 2 - 1:
            c_copy(1, h).wait_send()
    for d in range(1, NY):
        d_copy(d).wait_send()
        vy_copy(d).wait_send()
        cy_copy(d).wait_send()
        pr_copy(d).wait_send()
        for a in range(ACT):
            l_copy(a, d).wait_send()
            ky_copy(a, d).wait_send()
    for a in range(ACT):

        def kz_sent(d, _, a=a):
            kz_copy(a, d).wait_send()
            return 0

        lax.fori_loop(1, NZ, kz_sent, 0)


def on_device(
    particles,
    velocities,
    cell_table,
    top_cells,
    active_ids,
    active_count,
    cell_requests,
    cell_lists,
    leaf_requests,
    leaf_lists,
    targets,
):
    speeds = jnp.transpose(velocities, (1, 0, 2))
    cells = jnp.pad(cell_table.T, ((0, 0), (0, 6))).reshape(32, 128)
    top = jnp.pad(top_cells, ((0, 6), (0, 64)))
    vmem = pl.BlockSpec(memory_space=pltpu.VMEM)
    smem = pl.BlockSpec(memory_space=pltpu.SMEM)
    f32 = jnp.float32
    dma = pltpu.SemaphoreType.DMA
    placed, moved = pl.pallas_call(
        kernel,
        out_shape=(
            jax.ShapeDtypeStruct((NB, 4, 512), f32),
            jax.ShapeDtypeStruct((3, NB, 512), f32),
        ),
        in_specs=[vmem] * 4 + [smem] * 7,
        out_specs=(vmem, vmem),
        scratch_shapes=[
            pltpu.VMEM((NZ, NB, 4, 512), f32),
            pltpu.VMEM((NZ, 3, NB, 512), f32),
            pltpu.VMEM((NY, 3, NB, 512), f32),
            pltpu.VMEM((NY * NZ, 32, 128), f32),
            pltpu.VMEM((NL, 16, 128), f32),
            pltpu.VMEM((16, 512), f32),
            pltpu.VMEM((NY, 8, 128), jnp.int32),
            pltpu.SMEM((NY, 8, 128), jnp.int32),
            pltpu.VMEM((NY - 1, ACT, LPER, 4, 512), f32),
        ]
        + [pltpu.VMEM((NY, LPER, 4, 512), f32)] * ACT
        + [pltpu.VMEM((NY, NZ, 4, 512), f32)] * ACT
        + [
            pltpu.VMEM((NY, NB, 4, 512), f32),
            pltpu.VMEM((ACT, 3, 512, 128), f32),
            pltpu.VMEM((ACT, 3, 512, 128), f32),
            pltpu.VMEM((ACT, 8, 512), f32),
            pltpu.VMEM((ACT * CPER, 128), f32),
            pltpu.VMEM((ACT * CPER, 128), jnp.int32),
            pltpu.VMEM((128, ACT * CPER), f32),
            dma((2, 8, SUBS)),
            dma((2, 8, SUBS)),
            dma((2, 8)),
            dma((2, 8)),
            dma((2, 8, 3)),
            dma((2, 8, 3)),
            dma((NL,)),
            dma((NL,)),
            dma((NY,)),
            dma((NY,)),
            dma((NY,)),
            dma((NY,)),
            dma((NY,)),
            dma((NY,)),
            dma((ACT, NY)),
            dma((ACT, NY)),
            dma((NY,)),
            dma((NY,)),
            dma((ACT, NZ)),
            dma((ACT, NZ)),
            dma((ACT, NY)),
            dma((ACT, NY)),
            dma((5,)),
        ],
        compiler_params=pltpu.CompilerParams(
            collective_id=0, has_side_effects=True, vmem_limit_bytes=56 * 1024 * 1024
        ),
    )(
        particles,
        speeds,
        cells,
        top,
        active_ids,
        active_count,
        cell_lists,
        cell_requests[0].T,
        leaf_requests[0].T,
        leaf_lists,
        targets,
    )
    return placed, jnp.transpose(moved, (1, 0, 2))


def solution(mesh):
    placed = (
        P(("leaf", "bulk"), None, None),
        P(("leaf", "bulk"), None, None),
        P(None, ("leaf", "bulk")),
        P(None, "leaf"),
        P(("leaf", "bulk")),
        P(("leaf", "bulk")),
        P(("leaf", "bulk"), None, None),
        P(("leaf", "bulk"), None),
        P(("leaf", "bulk"), None, None),
        P(("leaf", "bulk"), None),
        P(("leaf", "bulk")),
    )
    return jax.shard_map(
        on_device,
        mesh=mesh,
        in_specs=placed,
        out_specs=(P(("leaf", "bulk"), None, None), P(("leaf", "bulk"), None, None)),
        check_vma=False,
    )
```

```python
import functools

import jax
import jax.numpy as jnp
from jax import lax
from jax.experimental import pallas as pl
from jax.experimental.pallas import tpu as pltpu
from jax.sharding import PartitionSpec as P

MESH = pl.DeviceIdType.MESH
step_time = 0.5
pair_soft = 0.01
cell_soft = 1.0

NY, NZ, NL = 4, 16, 8
NB = 32
ACT = 4
LPER = 6
CPER = 64
SUBS = 4
SROW = NB // SUBS
OCT = 64


def pair_terms(px, py, pz, src, accs):
    ax, ay, az = accs
    for sx, sy, sz, sm in src:
        dx = sx - px
        dy = sy - py
        dz = sz - pz
        inv = lax.rsqrt(dx * dx + dy * dy + (dz * dz + pair_soft))
        w = sm * inv * (inv * inv)
        ax = ax + w * dx
        ay = ay + w * dy
        az = az + w * dz
    return ax, ay, az


def cell_terms(px, py, pz, cells, accs):
    ax, ay, az = accs
    for m, cx, cy, cz, xx, yy, zz, xy, xz, yz in cells:
        dx = px - cx
        dy = py - cy
        dz = pz - cz
        inv = lax.rsqrt(dx * dx + dy * dy + (dz * dz + cell_soft))
        inv2 = inv * inv
        inv3 = inv2 * inv
        inv5 = inv3 * inv2
        tx = xx * dx + xy * dy + xz * dz
        ty = xy * dx + yy * dy + yz * dz
        tz = xz * dx + yz * dy + zz * dz
        u = dx * tx + dy * ty + dz * tz
        rad = m * inv3 + (2.5 * u) * (inv5 * inv2)
        ax = ax + (tx * inv5 - rad * dx)
        ay = ay + (ty * inv5 - rad * dy)
        az = az + (tz * inv5 - rad * dz)
    return ax, ay, az


def kernel(
    part, vel, cells, top, act_ids, act_cnt, cell_lists, cell_req, leaf_req, leaf_lists, targets,
    outp, outv,
    p_all, v_all, v_y, c_all, t_all, top_m, codes_v, codes_s, l_send,
    l0, l1, l2, l3, k0, k1, k2, k3, p_rec, pts, acc, own, near,
    p_ss, p_rs, c_ss, c_rs, v_ss, v_rs, t_ss, t_rs, d_ss, d_rs, vy_ss, vy_rs,
    cy_ss, cy_rs, l_ss, l_rs, pr_ss, pr_rs, kz_ss, kz_rs, ky_ss, ky_rs, loc,
):
    l_rec = (l0, l1, l2, l3)
    k_all = (k0, k1, k2, k3)
    leaf = lax.axis_index("leaf")
    bulk = lax.axis_index("bulk")
    y = bulk // NZ
    z = bulk % NZ

    def row_peer(d):
        return y * NZ + (z + d) % NZ

    def col_peer(d):
        return ((y + d) % NY) * NZ + z

    own_p = pltpu.make_async_copy(part, p_all.at[z], loc.at[0])
    own_v = pltpu.make_async_copy(vel, v_y.at[pl.ds(y * 3, 3)], loc.at[1])
    own_p.start()
    own_v.start()
    c_all[bulk, pl.ds(0, 8), :] = cells[pl.ds(0, 8), :]
    c_all[bulk, pl.ds(8, 8), :] = jnp.concatenate(
        [cells[pl.ds(8, 2), :], jnp.zeros((6, 256), jnp.float32)], axis=0
    )
    t_all[leaf] = jnp.zeros((16, 128), jnp.float32)
    t_all[leaf, pl.ds(0, 10), pl.ds(0, 64)] = top[...]

    def code_of(a, e):
        f = leaf_lists[a, e]
        peer = f // LCAP
        return peer * NB + leaf_req[f % LCAP, peer]

    LCAP = 2
    rows = lax.broadcasted_iota(jnp.int32, (8, 128), 0)
    lanes = lax.broadcasted_iota(jnp.int32, (8, 128), 1)
    code = jnp.zeros((8, 128), jnp.int32)
    for a in range(ACT):
        for e in range(LPER):
            code = jnp.where((rows == a) & (lanes == e), code_of(a, e), code)
    codes_v[y] = code

    barrier = pltpu.get_barrier_semaphore()

    def greet(dev):
        pl.semaphore_signal(barrier, inc=1, device_id=dev, device_id_type=MESH)

    for d in (1, 2, NZ - 2, NZ - 1):
        greet({"bulk": row_peer(d)})
    for d in range(1, NY):
        greet({"bulk": col_peer(d)})
    for d in range(1, NL):
        greet({"leaf": (leaf + d) % NL})
    pl.semaphore_wait(barrier, 4 + NY + NL - 2)

    def remote(src, dst, ss, rs, dev):
        return pltpu.make_async_remote_copy(
            src_ref=src, dst_ref=dst, send_sem=ss, recv_sem=rs, device_id=dev, device_id_type=MESH
        )

    def ring_dev(way):
        return {"bulk": row_peer(1 if way == 0 else NZ - 1)}

    def ring_src(way, h):
        return (z + NZ - h) % NZ if way == 0 else (z + h) % NZ

    def p_copy(way, h, sub, first=False):
        at = ring_src(way, h)
        cut = pl.ds(sub * SROW, SROW)
        dst = p_all.at[at, cut]
        src = part.at[cut] if first else dst
        return remote(src, dst, p_ss.at[way, h, sub], p_rs.at[way, h, sub], ring_dev(way))

    def c_copy(way, h):
        at = c_all.at[y * NZ + ring_src(way, h)]
        return remote(at, at, c_ss.at[way, h], c_rs.at[way, h], ring_dev(way))

    def v_copy(way, h, sub):
        at = v_all.at[ring_src(way, h), sub]
        return remote(at, at, v_ss.at[way, h, sub], v_rs.at[way, h, sub], ring_dev(way))

    def t_copy(d):
        return remote(t_all.at[leaf], t_all.at[leaf], t_ss.at[d], t_rs.at[d], {"leaf": (leaf + d) % NL})

    def d_copy(d):
        return remote(
            codes_v.at[y], codes_v.at[y], d_ss.at[d], d_rs.at[d], {"bulk": col_peer(d)}
        )

    def y_gather(ref, size, ss, rs, k):
        half = (size + 1) // 2
        if k < 2:
            cut = ref.at[pl.ds(y * size, size)]
        elif k == 2:
            cut = ref.at[pl.ds(((y + NY - 1) % NY) * size, half)]
        else:
            cut = ref.at[pl.ds(((y + 1) % NY) * size + half, size - half)]
        return remote(cut, cut, ss, rs, {"bulk": col_peer(1 if k % 2 == 0 else NY - 1)})

    def vy_copy(k):
        return y_gather(v_y, 3, vy_ss.at[k], vy_rs.at[k], k)

    def cy_copy(k):
        return y_gather(c_all, NZ, cy_ss.at[k], cy_rs.at[k], k)

    def l_copy(a, d):
        return remote(
            l_send.at[d - 1, a], l_rec[a].at[y], l_ss.at[a, d], l_rs.at[a, d],
            {"bulk": col_peer(d)},
        )

    def pr_copy(k):
        return y_gather(p_rec, NB, pr_ss.at[k], pr_rs.at[k], k)

    def ky_copy(a, k):
        return y_gather(k_all[a], NZ, ky_ss.at[a, k], ky_rs.at[a, k], k)

    def kz_copy(a, dist):
        if dist <= NZ // 2:
            hop = 1 if dist == 1 else 2
            at, to = (z + NZ - (dist - hop)) % NZ, hop
        else:
            back = NZ - dist
            hop = 1 if back == 1 else 2
            at, to = (z + (back - hop)) % NZ, NZ - hop
        cut = k_all[a].at[y * NZ + at]
        return remote(cut, cut, kz_ss.at[a, dist], kz_rs.at[a, dist], {"bulk": row_peer(to)})

    def k_start(a):
        for dist in (1, NZ - 1, 2, NZ - 2):
            kz_copy(a, dist).start()

    def k_step(a, step):
        for dist in (2 * step - 1, NZ - 2 * step + 1, 2 * step, NZ - 2 * step):
            kz_copy(a, dist).wait_recv()
        sends = [2 * step + 1, NZ - 2 * step - 1, 2 * step + 2]
        if step < NZ // 4 - 1:
            sends.append(NZ - 2 * step - 2)
        for dist in sends:
            kz_copy(a, dist).start()

    def y_send(a):
        for dist in (NZ // 2 - 1, NZ // 2, NZ // 2 + 1):
            kz_copy(a, dist).wait_recv()
        for k in range(2):
            ky_copy(a, k).start()

    def y_forward(copy):
        for k in range(2):
            copy(k).wait_recv()
        for k in range(2, 4):
            copy(k).start()

    def y_done(copy):
        for k in range(2, 4):
            copy(k).wait_recv()

    for d in range(1, NL):
        t_copy(d).start()
    for way in range(2):
        c_copy(way, 0).start()
    for d in range(1, NY):
        d_copy(d).start()
    for sub in range(SUBS):
        for way in range(2):
            p_copy(way, 0, sub, True).start()
    own_v.wait()
    for k in range(2):
        vy_copy(k).start()

    for a in range(ACT):
        bucket = part[act_ids[a]]
        own[a, pl.ds(0, 4), :] = bucket

        def spread(c, _, a=a):
            row = own[a, pl.ds(c, 1), :]
            pts[a, c] = jnp.transpose(jnp.broadcast_to(row, (128, 512)))
            return 0

        lax.fori_loop(0, 3, spread, 0)

    for d in range(1, NL):
        t_copy(d).wait_recv()
    half = lax.broadcasted_iota(jnp.int32, (16, 128), 1) < 64
    for i in range(4):
        top_m[:, pl.ds(i * 128, 128)] = jnp.where(
            half, t_all[2 * i], pltpu.roll(t_all[2 * i + 1], 64, 1)
        )

    def src_rows(load, tiles=4):
        out = []
        for i in range(tiles):
            sx, sy, sz, sm = [load(c, pl.ds(i * 128, 128)) for c in range(4)]
            out.append((sx, sy, sz, sm * (1.0 / (512.0 * (LPER + 1)))))
        return out

    def self_top(a, o0, count):
        src = src_rows(lambda c, cut: own[a, pl.ds(c, 1), cut])

        def step(i, _):
            at = pl.ds(pl.multiple_of((o0 + i) * 8, 8), 8)
            px, py, pz = pts[a, 0, at, :], pts[a, 1, at, :], pts[a, 2, at, :]
            zero = jnp.zeros((8, 128), jnp.float32)
            accs = pair_terms(px, py, pz, src, (zero, zero, zero))
            tops = [
                [top_m[pl.ds(k, 1), pl.ds(j * 128, 128)] for k in range(10)] for j in range(4)
            ]
            accs = cell_terms(px, py, pz, tops, accs)
            for c in range(3):
                acc[a, c, at, :] = accs[c]
            return 0

        lax.fori_loop(0, count, step, 0, unroll=2)

    def near_part(a, o0, count):
        cut = pl.ds(pl.multiple_of((a // 2) * 128, 128), 128)
        lane = lax.broadcasted_iota(jnp.int32, (1, 128), 1)
        mine = (lane // CPER) == (a % 2)
        cell = [near[pl.ds(k, 1), cut] for k in range(10)]
        cell = [v if 1 <= k <= 3 else jnp.where(mine, v, 0.0) for k, v in enumerate(cell)]

        def step(i, _):
            at = pl.ds(pl.multiple_of((o0 + i) * 8, 8), 8)
            px, py, pz = pts[a, 0, at, :], pts[a, 1, at, :], pts[a, 2, at, :]
            accs = tuple(acc[a, c, at, :] for c in range(3))
            accs = cell_terms(px, py, pz, [cell], accs)
            for c in range(3):
                acc[a, c, at, :] = accs[c]
            return 0

        lax.fori_loop(0, count, step, 0, unroll=4)

    def p_event(i):
        h = i // SUBS
        sub = i % SUBS
        for way in range(2):
            mine = (sub < SUBS // 2) if way == 0 else (sub >= SUBS // 2)

            @pl.when((h < NZ // 2 - 1) | mine)
            def _():
                p_copy(way, h, sub).wait_recv()

            @pl.when((h < NZ // 2 - 2) | ((h == NZ // 2 - 2) & mine))
            def _():
                p_copy(way, h + 1, sub).start()

    def c_event(i):
        for way in range(2):
            if way == 0:
                c_copy(way, i).wait_recv()

                @pl.when(i < NZ // 2 - 1)
                def _():
                    c_copy(way, i + 1).start()
            else:

                @pl.when(i < NZ // 2 - 1)
                def _():
                    c_copy(way, i).wait_recv()

                @pl.when(i < NZ // 2 - 2)
                def _():
                    c_copy(way, i + 1).start()

    def first_events(i, _):
        c_event(i)
        p_event(i)
        self_top(i // 8, (i % 8) * 8, 8)
        return 0

    lax.fori_loop(0, 8, first_events, 0)
    y_forward(vy_copy)
    for k in range(2):
        cy_copy(k).start()

    def more_events(i, _):
        p_event(i)
        self_top(i // 8, (i % 8) * 8, 8)
        return 0

    lax.fori_loop(8, 16, more_events, 0)

    y_done(vy_copy)
    y_forward(cy_copy)

    def pick_row(j, _):
        shift = (targets[j] - bulk) & 63
        to_z = (z + shift) & 15
        from_y = ((y * NZ + to_z - shift) & 63) >> 4
        for c in range(3):
            v_all[z, c, pl.ds(j, 1), :] = v_y[from_y * 3 + c, pl.ds(j, 1), :]
        return 0

    lax.fori_loop(0, NB, pick_row, 0, unroll=8)
    lax.fori_loop(16, 24, more_events, 0)

    y_done(cy_copy)
    lane16 = lax.broadcasted_iota(jnp.int32, (16, 128), 1)
    lane256 = lax.broadcasted_iota(jnp.int32, (16, 256), 1)
    for part_at in range(2):

        def pick_cell(i, got, part_at=part_at):
            f = cell_lists[part_at * 2 + i // CPER, i % CPER]
            peer = f >> 4
            col = cell_req[f & 15, peer] & 255
            one = jnp.where(lane256 == col, c_all[peer], 0.0)
            return jnp.where(lane16 == i, jnp.sum(one, axis=1, keepdims=True), got)

        near[:, pl.ds(part_at * 128, 128)] = lax.fori_loop(
            0, 128, pick_cell, jnp.zeros((16, 128), jnp.float32), unroll=8
        )

    def last_events(i, _):
        p_event(i)
        self_top(i // 8, (i % 8) * 8, 8)
        near_part((i - 24) // 2, (i % 2) * (OCT // 2), OCT // 2)
        return 0

    lax.fori_loop(24, 32, last_events, 0)

    own_p.wait()
    for d in range(1, NY):
        d_copy(d).wait_recv()
    codes_copy = pltpu.make_async_copy(codes_v, codes_s, loc.at[2])
    codes_copy.start()
    codes_copy.wait()

    def leaf_at(number):
        return p_all[(number >> 5) & 15, number & 31]

    for a in range(ACT):
        for d in range(1, NY):
            to_y = (y + d) % NY

            def fill(e, _, a=a, d=d, to_y=to_y):
                l_send[d - 1, a, e] = leaf_at(codes_s[to_y, a, e])
                return 0

            lax.fori_loop(0, LPER, fill, 0, unroll=True)
            l_copy(a, d).start()

        def fill_own(e, _, a=a):
            l_rec[a][y, e] = leaf_at(code_of(a, e))
            return 0

        lax.fori_loop(0, LPER, fill_own, 0, unroll=True)

    for way in range(2):
        for sub in range(3):
            v_copy(way, 0, sub).start()

    def pick_moved(j, _):
        from_z = (bulk - (targets[j] - bulk)) & 15
        p_rec[y * NB + j] = p_all[from_z, j]
        return 0

    lax.fori_loop(0, NB, pick_moved, 0, unroll=8)
    for k in range(2):
        pr_copy(k).start()

    def v_event(i):
        h = i // 3
        sub = i % 3
        for way in range(2):
            mine = (sub == 0) if way == 0 else (sub > 0)

            @pl.when((h < NZ // 2 - 1) | mine)
            def _():
                v_copy(way, h, sub).wait_recv()

            @pl.when((h < NZ // 2 - 2) | ((h == NZ // 2 - 2) & mine))
            def _():
                v_copy(way, h + 1, sub).start()

    for a in range(ACT):
        for d in range(1, NY):
            l_copy(a, d).wait_recv()
        if a >= 2:
            y_send(a - 2)
        if a == 3:
            y_forward(pr_copy)

        def block(e, _, a=a):
            from_y = (code_of(a, e) >> 9) & 3
            src = src_rows(lambda c, cut: l_rec[a][from_y, e, pl.ds(c, 1), cut])

            def step(i, _):
                at = pl.ds(pl.multiple_of(i * 8, 8), 8)
                px, py, pz = pts[a, 0, at, :], pts[a, 1, at, :], pts[a, 2, at, :]
                accs = tuple(acc[a, c, at, :] for c in range(3))
                accs = pair_terms(px, py, pz, src, accs)
                for c in range(3):
                    acc[a, c, at, :] = accs[c]
                return 0

            lax.fori_loop(0, OCT, step, 0, unroll=4)

            @pl.when(e % 2 == 0)
            def _():
                v_event(a * 3 + e // 2)

            if a >= 1:
                for step_at in (1, 2, 3):

                    @pl.when(e == 2 * step_at - 1)
                    def _(step_at=step_at):
                        k_step(a - 1, step_at)

            if a >= 2:

                @pl.when(e == 4)
                def _():
                    y_forward(functools.partial(ky_copy, a - 2))

            return 0

        lax.fori_loop(0, LPER, block, 0)
        alive = jnp.where(a < act_cnt[0], 1.0, 0.0)
        ident = jnp.where(a < act_cnt[0], act_ids[a], -1).astype(jnp.float32)
        for c in range(3):
            pull = jnp.sum(jnp.transpose(acc[a, c]), axis=0, keepdims=True)
            k_all[a][bulk, pl.ds(c, 1), :] = step_time * pull * alive
        k_all[a][bulk, pl.ds(3, 1), :] = jnp.full((1, 512), ident, jnp.float32)

        k_start(a)

    last = ACT - 1
    y_send(last - 1)
    v_event(12)
    k_step(last, 1)
    v_event(13)
    k_step(last, 2)
    y_forward(functools.partial(ky_copy, last - 1))
    v_event(14)
    k_step(last, 3)
    v_event(15)
    y_send(last)
    v_event(16)
    v_event(17)
    y_forward(functools.partial(ky_copy, last))

    def tail_events(i, _):
        v_event(i)
        return 0

    lax.fori_loop(18, 24, tail_events, 0)
    y_done(pr_copy)
    for a in range(ACT):
        y_done(functools.partial(ky_copy, a))

    def place(j, _):
        source = (bulk - (targets[j] - bulk)) & 63
        from_y = source >> 4
        from_z = source & 15
        number = j.astype(jnp.float32)
        hits = [k_all[a][source, pl.ds(3, 1), :] == number for a in range(ACT)]
        for c in range(3):
            speed = v_all[from_z, c, pl.ds(j, 1), :]
            kick = jnp.zeros((1, 512), jnp.float32)
            for a in range(ACT):
                kick = kick + jnp.where(
                    hits[a], k_all[a][source, pl.ds(c, 1), :], 0.0
                )
            speed = speed + kick
            outv[c, pl.ds(j, 1), :] = speed
            outp[j, pl.ds(c, 1), :] = p_rec[from_y * NB + j, pl.ds(c, 1), :] + step_time * speed
        outp[j, pl.ds(3, 1), :] = p_rec[from_y * NB + j, pl.ds(3, 1), :]
        return 0

    lax.fori_loop(0, NB, place, 0, unroll=4)

    for d in range(1, NL):
        t_copy(d).wait_send()

    def p_sent(i, _):
        h = i // SUBS
        sub = i % SUBS
        for way in range(2):
            mine = (sub < SUBS // 2) if way == 0 else (sub >= SUBS // 2)

            @pl.when((h < NZ // 2 - 1) | mine)
            def _():
                p_copy(way, h, sub).wait_send()

        return 0

    lax.fori_loop(0, 32, p_sent, 0)

    def v_sent(i, _):
        h = i // 3
        sub = i % 3
        for way in range(2):
            mine = (sub == 0) if way == 0 else (sub > 0)

            @pl.when((h < NZ // 2 - 1) | mine)
            def _():
                v_copy(way, h, sub).wait_send()

        return 0

    lax.fori_loop(0, 24, v_sent, 0)
    for h in range(NZ // 2):
        c_copy(0, h).wait_send()
        if h < NZ // 2 - 1:
            c_copy(1, h).wait_send()
    for d in range(1, NY):
        d_copy(d).wait_send()
        for a in range(ACT):
            l_copy(a, d).wait_send()
    for k in range(4):
        vy_copy(k).wait_send()
        cy_copy(k).wait_send()
        pr_copy(k).wait_send()
        for a in range(ACT):
            ky_copy(a, k).wait_send()
    for a in range(ACT):
        for dist in range(1, NZ):
            kz_copy(a, dist).wait_send()


def on_device(
    particles,
    velocities,
    cell_table,
    top_cells,
    active_ids,
    active_count,
    cell_requests,
    cell_lists,
    leaf_requests,
    leaf_lists,
    targets,
):
    speeds = jnp.transpose(velocities, (1, 0, 2))
    vmem = pl.BlockSpec(memory_space=pltpu.VMEM)
    smem = pl.BlockSpec(memory_space=pltpu.SMEM)
    f32 = jnp.float32
    dma = pltpu.SemaphoreType.DMA
    placed, moved = pl.pallas_call(
        kernel,
        out_shape=(
            jax.ShapeDtypeStruct((NB, 4, 512), f32),
            jax.ShapeDtypeStruct((3, NB, 512), f32),
        ),
        in_specs=[vmem] * 4 + [smem] * 7,
        out_specs=(vmem, vmem),
        scratch_shapes=[
            pltpu.VMEM((NZ, NB, 4, 512), f32),
            pltpu.VMEM((NZ, 3, NB, 512), f32),
            pltpu.VMEM((NY * 3, NB, 512), f32),
            pltpu.VMEM((NY * NZ, 16, 256), f32),
            pltpu.VMEM((NL, 16, 128), f32),
            pltpu.VMEM((16, 512), f32),
            pltpu.VMEM((NY, 8, 128), jnp.int32),
            pltpu.SMEM((NY, 8, 128), jnp.int32),
            pltpu.VMEM((NY - 1, ACT, LPER, 4, 512), f32),
        ]
        + [pltpu.VMEM((NY, LPER, 4, 512), f32)] * ACT
        + [pltpu.VMEM((NY * NZ, 4, 512), f32)] * ACT
        + [
            pltpu.VMEM((NY * NB, 4, 512), f32),
            pltpu.VMEM((ACT, 3, 512, 128), f32),
            pltpu.VMEM((ACT, 3, 512, 128), f32),
            pltpu.VMEM((ACT, 8, 512), f32),
            pltpu.VMEM((16, ACT * CPER), f32),
            dma((2, 8, SUBS)),
            dma((2, 8, SUBS)),
            dma((2, 8)),
            dma((2, 8)),
            dma((2, 8, 3)),
            dma((2, 8, 3)),
            dma((NL,)),
            dma((NL,)),
            dma((NY,)),
            dma((NY,)),
            dma((NY,)),
            dma((NY,)),
            dma((NY,)),
            dma((NY,)),
            dma((ACT, NY)),
            dma((ACT, NY)),
            dma((NY,)),
            dma((NY,)),
            dma((ACT, NZ)),
            dma((ACT, NZ)),
            dma((ACT, NY)),
            dma((ACT, NY)),
            dma((5,)),
        ],
        compiler_params=pltpu.CompilerParams(
            collective_id=0, has_side_effects=True, vmem_limit_bytes=56 * 1024 * 1024
        ),
    )(
        particles,
        speeds,
        cell_table,
        top_cells,
        active_ids,
        active_count,
        cell_lists,
        cell_requests[0].T,
        leaf_requests[0].T,
        leaf_lists,
        targets,
    )
    return placed, jnp.transpose(moved, (1, 0, 2))


def solution(mesh):
    placed = (
        P(("leaf", "bulk"), None, None),
        P(("leaf", "bulk"), None, None),
        P(None, ("leaf", "bulk")),
        P(None, "leaf"),
        P(("leaf", "bulk")),
        P(("leaf", "bulk")),
        P(("leaf", "bulk"), None, None),
        P(("leaf", "bulk"), None),
        P(("leaf", "bulk"), None, None),
        P(("leaf", "bulk"), None),
        P(("leaf", "bulk")),
    )
    return jax.shard_map(
        on_device,
        mesh=mesh,
        in_specs=placed,
        out_specs=(P(("leaf", "bulk"), None, None), P(("leaf", "bulk"), None, None)),
        check_vma=False,
    )
```

```python
import functools

import jax
import jax.numpy as jnp
from jax import lax
from jax.experimental import pallas as pl
from jax.experimental.pallas import tpu as pltpu
from jax.sharding import PartitionSpec as P

MESH = pl.DeviceIdType.MESH
step_time = 0.5
pair_soft = 0.01
cell_soft = 1.0

NY, NZ, NL = 4, 16, 8
NB = 32
ACT = 4
LPER = 6
CPER = 64
SUBS = 4
SROW = NB // SUBS
OCT = 64


def pair_terms(px, py, pz, src, accs):
    ax, ay, az = accs
    for sx, sy, sz, sm in src:
        dx = sx - px
        dy = sy - py
        dz = sz - pz
        inv = lax.rsqrt(dx * dx + dy * dy + (dz * dz + pair_soft))
        w = sm * inv * (inv * inv)
        ax = ax + w * dx
        ay = ay + w * dy
        az = az + w * dz
    return ax, ay, az


def cell_terms(px, py, pz, cells, accs):
    ax, ay, az = accs
    for m, cx, cy, cz, xx, yy, zz, xy, xz, yz in cells:
        dx = px - cx
        dy = py - cy
        dz = pz - cz
        inv = lax.rsqrt(dx * dx + dy * dy + (dz * dz + cell_soft))
        inv2 = inv * inv
        inv3 = inv2 * inv
        inv5 = inv3 * inv2
        tx = xx * dx + xy * dy + xz * dz
        ty = xy * dx + yy * dy + yz * dz
        tz = xz * dx + yz * dy + zz * dz
        u = dx * tx + dy * ty + dz * tz
        rad = m * inv3 + (2.5 * u) * (inv5 * inv2)
        ax = ax + (tx * inv5 - rad * dx)
        ay = ay + (ty * inv5 - rad * dy)
        az = az + (tz * inv5 - rad * dz)
    return ax, ay, az


def kernel(
    part, vel, cells, top, act_ids, act_cnt, cell_lists, cell_req, leaf_req, leaf_lists, targets,
    outp, outv,
    p_all, v_all, v_y, c_all, t_all, top_m, codes_v, codes_s, l_send,
    l0, l1, l2, l3, k0, k1, k2, k3, p_rec, pts, acc, own, near,
    p_ss, p_rs, c_ss, c_rs, v_ss, v_rs, t_ss, t_rs, d_ss, d_rs, vy_ss, vy_rs,
    cy_ss, cy_rs, l_ss, l_rs, pr_ss, pr_rs, kz_ss, kz_rs, ky_ss, ky_rs, loc,
):
    l_rec = (l0, l1, l2, l3)
    k_all = (k0, k1, k2, k3)
    leaf = lax.axis_index("leaf")
    bulk = lax.axis_index("bulk")
    y = bulk // NZ
    z = bulk % NZ

    def row_peer(d):
        return y * NZ + (z + d) % NZ

    def col_peer(d):
        return ((y + d) % NY) * NZ + z

    def ident_of(a):
        return jnp.where(a < act_cnt[0], act_ids[a], -1).astype(jnp.float32)

    own_p = pltpu.make_async_copy(part, p_all.at[z], loc.at[0])
    own_v = pltpu.make_async_copy(vel, v_y.at[pl.ds(y * 3, 3)], loc.at[1])
    own_p.start()
    own_v.start()
    c_all[bulk, pl.ds(0, 8), :] = cells[pl.ds(0, 8), :]
    c_all[bulk, pl.ds(8, 8), :] = jnp.concatenate(
        [cells[pl.ds(8, 2), :]]
        + [jnp.full((1, 256), ident_of(a), jnp.float32) for a in range(ACT)]
        + [jnp.zeros((2, 256), jnp.float32)],
        axis=0,
    )
    t_all[leaf] = jnp.zeros((16, 128), jnp.float32)
    t_all[leaf, pl.ds(0, 10), pl.ds(0, 64)] = top[...]

    def code_of(a, e):
        f = leaf_lists[a, e]
        peer = f // LCAP
        return peer * NB + leaf_req[f % LCAP, peer]

    LCAP = 2
    rows = lax.broadcasted_iota(jnp.int32, (8, 128), 0)
    lanes = lax.broadcasted_iota(jnp.int32, (8, 128), 1)
    code = jnp.zeros((8, 128), jnp.int32)
    for a in range(ACT):
        for e in range(LPER):
            code = jnp.where((rows == a) & (lanes == e), code_of(a, e), code)
    codes_v[y] = code

    barrier = pltpu.get_barrier_semaphore()

    def greet(dev):
        pl.semaphore_signal(barrier, inc=1, device_id=dev, device_id_type=MESH)

    for d in (1, 2, 4, 8, NZ - 4, NZ - 2, NZ - 1):
        greet({"bulk": row_peer(d)})
    for d in range(1, NY):
        greet({"bulk": col_peer(d)})
    for d in range(1, NL):
        greet({"leaf": (leaf + d) % NL})
    pl.semaphore_wait(barrier, 7 + NY + NL - 2)

    def remote(src, dst, ss, rs, dev):
        return pltpu.make_async_remote_copy(
            src_ref=src, dst_ref=dst, send_sem=ss, recv_sem=rs, device_id=dev, device_id_type=MESH
        )

    def ring_dev(way):
        return {"bulk": row_peer(1 if way == 0 else NZ - 1)}

    def ring_src(way, h):
        return (z + NZ - h) % NZ if way == 0 else (z + h) % NZ

    def p_copy(way, h, sub, first=False):
        at = ring_src(way, h)
        cut = pl.ds(sub * SROW, SROW)
        dst = p_all.at[at, cut]
        src = part.at[cut] if first else dst
        return remote(src, dst, p_ss.at[way, h, sub], p_rs.at[way, h, sub], ring_dev(way))

    def c_copy(way, h):
        at = c_all.at[y * NZ + ring_src(way, h)]
        return remote(at, at, c_ss.at[way, h], c_rs.at[way, h], ring_dev(way))

    def v_copy(way, h, sub):
        at = v_all.at[ring_src(way, h), sub]
        return remote(at, at, v_ss.at[way, h, sub], v_rs.at[way, h, sub], ring_dev(way))

    def t_copy(d):
        return remote(t_all.at[leaf], t_all.at[leaf], t_ss.at[d], t_rs.at[d], {"leaf": (leaf + d) % NL})

    def d_copy(d):
        return remote(
            codes_v.at[y], codes_v.at[y], d_ss.at[d], d_rs.at[d], {"bulk": col_peer(d)}
        )

    def y_gather(ref, size, ss, rs, k):
        half = (size + 1) // 2
        if k < 2:
            cut = ref.at[pl.ds(y * size, size)]
        elif k == 2:
            cut = ref.at[pl.ds(((y + NY - 1) % NY) * size, half)]
        else:
            cut = ref.at[pl.ds(((y + 1) % NY) * size + half, size - half)]
        return remote(cut, cut, ss, rs, {"bulk": col_peer(1 if k % 2 == 0 else NY - 1)})

    def vy_copy(k):
        return y_gather(v_y, 3, vy_ss.at[k], vy_rs.at[k], k)

    def cy_copy(k):
        return y_gather(c_all, NZ, cy_ss.at[k], cy_rs.at[k], k)

    def l_copy(a, d):
        return remote(
            l_send.at[d - 1, a], l_rec[a].at[y], l_ss.at[a, d], l_rs.at[a, d],
            {"bulk": col_peer(d)},
        )

    def pr_copy(k):
        return y_gather(p_rec, NB, pr_ss.at[k], pr_rs.at[k], k)

    def ky_copy(a, d):
        cut = k_all[a].at[pl.ds(y * NZ, NZ)]
        return remote(cut, cut, ky_ss.at[a, d], ky_rs.at[a, d], {"bulk": col_peer(d)})

    far = (4, 8, 12)
    close = (1, NZ - 1, 2)

    def kz_copy(a, hop, base=0):
        cut = k_all[a].at[y * NZ + (z + NZ - base) % NZ]
        dist = (base + hop) % NZ
        return remote(cut, cut, kz_ss.at[a, dist], kz_rs.at[a, dist], {"bulk": row_peer(hop)})

    def k_far(a):
        for hop in (8, 4, 12):
            kz_copy(a, hop).start()
        for hop in close:
            kz_copy(a, hop).start()

    def k_close(a):
        for base in far:
            kz_copy(a, base).wait_recv()
            for hop in close:
                kz_copy(a, hop, base).start()

    def y_send(a):
        for base in (0,) + far:
            for hop in close:
                kz_copy(a, hop, base).wait_recv()
        for d in (2, 1, 3):
            ky_copy(a, d).start()

    def y_forward(copy):
        for k in range(2):
            copy(k).wait_recv()
        for k in range(2, 4):
            copy(k).start()

    def y_done(copy):
        for k in range(2, 4):
            copy(k).wait_recv()

    for d in range(1, NL):
        t_copy(d).start()
    for way in range(2):
        c_copy(way, 0).start()
    for d in range(1, NY):
        d_copy(d).start()
    for sub in range(SUBS):
        for way in range(2):
            p_copy(way, 0, sub, True).start()
    own_v.wait()
    for k in range(2):
        vy_copy(k).start()

    for a in range(ACT):
        bucket = part[act_ids[a]]
        own[a, pl.ds(0, 4), :] = bucket

        def spread(c, _, a=a):
            row = own[a, pl.ds(c, 1), :]
            pts[a, c] = jnp.transpose(jnp.broadcast_to(row, (128, 512)))
            return 0

        lax.fori_loop(0, 3, spread, 0)

    for d in range(1, NL):
        t_copy(d).wait_recv()
    half = lax.broadcasted_iota(jnp.int32, (16, 128), 1) < 64
    for i in range(4):
        top_m[:, pl.ds(i * 128, 128)] = jnp.where(
            half, t_all[2 * i], pltpu.roll(t_all[2 * i + 1], 64, 1)
        )

    def src_rows(load, tiles=4):
        out = []
        for i in range(tiles):
            sx, sy, sz, sm = [load(c, pl.ds(i * 128, 128)) for c in range(4)]
            out.append((sx, sy, sz, sm * (1.0 / (512.0 * (LPER + 1)))))
        return out

    def self_top(a, o0, count):
        src = src_rows(lambda c, cut: own[a, pl.ds(c, 1), cut])

        def step(i, _):
            at = pl.ds(pl.multiple_of((o0 + i) * 8, 8), 8)
            px, py, pz = pts[a, 0, at, :], pts[a, 1, at, :], pts[a, 2, at, :]
            zero = jnp.zeros((8, 128), jnp.float32)
            accs = pair_terms(px, py, pz, src, (zero, zero, zero))
            tops = [
                [top_m[pl.ds(k, 1), pl.ds(j * 128, 128)] for k in range(10)] for j in range(4)
            ]
            accs = cell_terms(px, py, pz, tops, accs)
            for c in range(3):
                acc[a, c, at, :] = accs[c]
            return 0

        lax.fori_loop(0, count, step, 0, unroll=2)

    def near_part(a, o0, count):
        cut = pl.ds(pl.multiple_of((a // 2) * 128, 128), 128)
        lane = lax.broadcasted_iota(jnp.int32, (1, 128), 1)
        mine = (lane // CPER) == (a % 2)
        cell = [near[pl.ds(k, 1), cut] for k in range(10)]
        cell = [v if 1 <= k <= 3 else jnp.where(mine, v, 0.0) for k, v in enumerate(cell)]

        def step(i, _):
            at = pl.ds(pl.multiple_of((o0 + i) * 8, 8), 8)
            px, py, pz = pts[a, 0, at, :], pts[a, 1, at, :], pts[a, 2, at, :]
            accs = tuple(acc[a, c, at, :] for c in range(3))
            accs = cell_terms(px, py, pz, [cell], accs)
            for c in range(3):
                acc[a, c, at, :] = accs[c]
            return 0

        lax.fori_loop(0, count, step, 0, unroll=4)

    def p_event(i):
        h = i // SUBS
        sub = i % SUBS
        for way in range(2):
            mine = (sub < SUBS // 2) if way == 0 else (sub >= SUBS // 2)

            @pl.when((h < NZ // 2 - 1) | mine)
            def _():
                p_copy(way, h, sub).wait_recv()

            @pl.when((h < NZ // 2 - 2) | ((h == NZ // 2 - 2) & mine))
            def _():
                p_copy(way, h + 1, sub).start()

    def c_event(i):
        for way in range(2):
            if way == 0:
                c_copy(way, i).wait_recv()

                @pl.when(i < NZ // 2 - 1)
                def _():
                    c_copy(way, i + 1).start()
            else:

                @pl.when(i < NZ // 2 - 1)
                def _():
                    c_copy(way, i).wait_recv()

                @pl.when(i < NZ // 2 - 2)
                def _():
                    c_copy(way, i + 1).start()

    def first_events(i, _):
        c_event(i)
        p_event(i)
        self_top(i // 8, (i % 8) * 8, 8)
        return 0

    lax.fori_loop(0, 8, first_events, 0)
    y_forward(vy_copy)
    for k in range(2):
        cy_copy(k).start()

    def more_events(i, _):
        p_event(i)
        self_top(i // 8, (i % 8) * 8, 8)
        return 0

    lax.fori_loop(8, 16, more_events, 0)

    y_done(vy_copy)
    y_forward(cy_copy)

    def pick_row(j, _):
        shift = (targets[j] - bulk) & 63
        to_z = (z + shift) & 15
        from_y = ((y * NZ + to_z - shift) & 63) >> 4
        for c in range(3):
            v_all[z, c, pl.ds(j, 1), :] = v_y[from_y * 3 + c, pl.ds(j, 1), :]
        return 0

    lax.fori_loop(0, NB, pick_row, 0, unroll=8)
    lax.fori_loop(16, 24, more_events, 0)

    y_done(cy_copy)
    lane16 = lax.broadcasted_iota(jnp.int32, (16, 128), 1)
    lane256 = lax.broadcasted_iota(jnp.int32, (16, 256), 1)
    for part_at in range(2):

        def pick_cell(i, got, part_at=part_at):
            f = cell_lists[part_at * 2 + i // CPER, i % CPER]
            peer = f >> 4
            col = cell_req[f & 15, peer] & 255
            one = jnp.where(lane256 == col, c_all[peer], 0.0)
            return jnp.where(lane16 == i, jnp.sum(one, axis=1, keepdims=True), got)

        near[:, pl.ds(part_at * 128, 128)] = lax.fori_loop(
            0, 128, pick_cell, jnp.zeros((16, 128), jnp.float32), unroll=8
        )

    def last_events(i, _):
        p_event(i)
        self_top(i // 8, (i % 8) * 8, 8)
        near_part((i - 24) // 2, (i % 2) * (OCT // 2), OCT // 2)
        return 0

    lax.fori_loop(24, 32, last_events, 0)

    own_p.wait()
    for d in range(1, NY):
        d_copy(d).wait_recv()
    codes_copy = pltpu.make_async_copy(codes_v, codes_s, loc.at[2])
    codes_copy.start()
    codes_copy.wait()

    def leaf_at(number):
        return p_all[(number >> 5) & 15, number & 31]

    for a in range(ACT):
        for d in range(1, NY):
            to_y = (y + d) % NY

            def fill(e, _, a=a, d=d, to_y=to_y):
                l_send[d - 1, a, e] = leaf_at(codes_s[to_y, a, e])
                return 0

            lax.fori_loop(0, LPER, fill, 0, unroll=True)
            l_copy(a, d).start()

        def fill_own(e, _, a=a):
            l_rec[a][y, e] = leaf_at(code_of(a, e))
            return 0

        lax.fori_loop(0, LPER, fill_own, 0, unroll=True)

    for way in range(2):
        for sub in range(3):
            v_copy(way, 0, sub).start()

    def pick_moved(j, _):
        from_z = (bulk - (targets[j] - bulk)) & 15
        p_rec[y * NB + j] = p_all[from_z, j]
        return 0

    lax.fori_loop(0, NB, pick_moved, 0, unroll=8)
    for k in range(2):
        pr_copy(k).start()

    def v_event(i):
        h = i // 3
        sub = i % 3
        for way in range(2):
            mine = (sub == 0) if way == 0 else (sub > 0)

            @pl.when((h < NZ // 2 - 1) | mine)
            def _():
                v_copy(way, h, sub).wait_recv()

            @pl.when((h < NZ // 2 - 2) | ((h == NZ // 2 - 2) & mine))
            def _():
                v_copy(way, h + 1, sub).start()

    for a in range(ACT):
        for d in range(1, NY):
            l_copy(a, d).wait_recv()
        if a == 3:
            y_forward(pr_copy)

        def block(e, _, a=a):
            from_y = (code_of(a, e) >> 9) & 3
            src = src_rows(lambda c, cut: l_rec[a][from_y, e, pl.ds(c, 1), cut])

            def step(i, _):
                at = pl.ds(pl.multiple_of(i * 8, 8), 8)
                px, py, pz = pts[a, 0, at, :], pts[a, 1, at, :], pts[a, 2, at, :]
                accs = tuple(acc[a, c, at, :] for c in range(3))
                accs = pair_terms(px, py, pz, src, accs)
                for c in range(3):
                    acc[a, c, at, :] = accs[c]
                return 0

            lax.fori_loop(0, OCT, step, 0, unroll=8)

            first = a * 4 - (a > 0)

            @pl.when(e % 2 == 1)
            def _():
                v_event(first + (a > 0) + e // 2)

            if a > 0:

                @pl.when(e == 0)
                def _():
                    v_event(first)

            if a >= 2:

                @pl.when(e == 3)
                def _():
                    k_close(a - 2)

            if a == 3:

                @pl.when(e == 2)
                def _():
                    y_send(0)

            return 0

        lax.fori_loop(0, LPER, block, 0)
        alive = jnp.where(a < act_cnt[0], step_time, 0.0)
        for c in range(3):
            pull = jnp.sum(jnp.transpose(acc[a, c]), axis=0, keepdims=True) * alive
            for b in range(4):
                row, col = divmod(c * 4 + b, 3)
                k_all[a][bulk, pl.ds(row, 1), pl.ds(col * 128, 128)] = pull[
                    :, b * 128 : (b + 1) * 128
                ]
        k_far(a)

    def v_events(lo, hi):
        def go(i, _):
            v_event(i)
            return 0

        lax.fori_loop(lo, hi, go, 0)

    for d in range(1, NL):
        t_copy(d).wait_send()

    def p_sent(i, _):
        h = i // SUBS
        sub = i % SUBS
        for way in range(2):
            mine = (sub < SUBS // 2) if way == 0 else (sub >= SUBS // 2)

            @pl.when((h < NZ // 2 - 1) | mine)
            def _():
                p_copy(way, h, sub).wait_send()

        return 0

    lax.fori_loop(0, 32, p_sent, 0)
    v_events(15, 16)
    y_send(1)
    v_events(16, 17)
    k_close(2)
    v_events(17, 18)
    for h in range(NZ // 2):
        c_copy(0, h).wait_send()
        if h < NZ // 2 - 1:
            c_copy(1, h).wait_send()
    for k in range(4):
        vy_copy(k).wait_send()
        cy_copy(k).wait_send()
    for d in range(1, NY):
        d_copy(d).wait_send()
        for a in range(ACT):
            l_copy(a, d).wait_send()
    v_events(18, 19)
    y_send(2)
    k_close(3)
    v_events(19, 21)
    y_done(pr_copy)
    for k in range(4):
        pr_copy(k).wait_send()
    y_send(3)
    v_events(21, 24)

    def v_sent(i, _):
        h = i // 3
        sub = i % 3
        for way in range(2):
            mine = (sub == 0) if way == 0 else (sub > 0)

            @pl.when((h < NZ // 2 - 1) | mine)
            def _():
                v_copy(way, h, sub).wait_send()

        return 0

    lax.fori_loop(0, 24, v_sent, 0)
    for a in range(ACT):
        for dist in range(1, NZ):
            kz_copy(a, dist).wait_send()
    for a in range(ACT):
        for d in range(1, NY):
            ky_copy(a, d).wait_recv()

    def place(j, _):
        source = (bulk - (targets[j] - bulk)) & 63
        from_y = source >> 4
        from_z = source & 15
        number = j.astype(jnp.float32)
        hits = [c_all[source, pl.ds(10 + a, 1), pl.ds(0, 128)] == number for a in range(ACT)]
        for c in range(3):
            parts = []
            for b in range(4):
                row, col = divmod(c * 4 + b, 3)
                kick = jnp.zeros((1, 128), jnp.float32)
                for a in range(ACT):
                    got = k_all[a][source, pl.ds(row, 1), pl.ds(col * 128, 128)]
                    kick = kick + jnp.where(hits[a], got, 0.0)
                parts.append(kick)
            speed = v_all[from_z, c, pl.ds(j, 1), :] + jnp.concatenate(parts, axis=1)
            outv[c, pl.ds(j, 1), :] = speed
            outp[j, pl.ds(c, 1), :] = p_rec[from_y * NB + j, pl.ds(c, 1), :] + step_time * speed
        outp[j, pl.ds(3, 1), :] = p_rec[from_y * NB + j, pl.ds(3, 1), :]
        return 0

    lax.fori_loop(0, NB, place, 0, unroll=4)

    for a in range(ACT):
        for d in range(1, NY):
            ky_copy(a, d).wait_send()


def on_device(
    particles,
    velocities,
    cell_table,
    top_cells,
    active_ids,
    active_count,
    cell_requests,
    cell_lists,
    leaf_requests,
    leaf_lists,
    targets,
):
    speeds = jnp.transpose(velocities, (1, 0, 2))
    vmem = pl.BlockSpec(memory_space=pltpu.VMEM)
    smem = pl.BlockSpec(memory_space=pltpu.SMEM)
    f32 = jnp.float32
    dma = pltpu.SemaphoreType.DMA
    placed, moved = pl.pallas_call(
        kernel,
        out_shape=(
            jax.ShapeDtypeStruct((NB, 4, 512), f32),
            jax.ShapeDtypeStruct((3, NB, 512), f32),
        ),
        in_specs=[vmem] * 4 + [smem] * 7,
        out_specs=(vmem, vmem),
        scratch_shapes=[
            pltpu.VMEM((NZ, NB, 4, 512), f32),
            pltpu.VMEM((NZ, 3, NB, 512), f32),
            pltpu.VMEM((NY * 3, NB, 512), f32),
            pltpu.VMEM((NY * NZ, 16, 256), f32),
            pltpu.VMEM((NL, 16, 128), f32),
            pltpu.VMEM((16, 512), f32),
            pltpu.VMEM((NY, 8, 128), jnp.int32),
            pltpu.SMEM((NY, 8, 128), jnp.int32),
            pltpu.VMEM((NY - 1, ACT, LPER, 4, 512), f32),
        ]
        + [pltpu.VMEM((NY, LPER, 4, 512), f32)] * ACT
        + [pltpu.VMEM((NY * NZ, 4, 384), f32)] * ACT
        + [
            pltpu.VMEM((NY * NB, 4, 512), f32),
            pltpu.VMEM((ACT, 3, 512, 128), f32),
            pltpu.VMEM((ACT, 3, 512, 128), f32),
            pltpu.VMEM((ACT, 8, 512), f32),
            pltpu.VMEM((16, ACT * CPER), f32),
            dma((2, 8, SUBS)),
            dma((2, 8, SUBS)),
            dma((2, 8)),
            dma((2, 8)),
            dma((2, 8, 3)),
            dma((2, 8, 3)),
            dma((NL,)),
            dma((NL,)),
            dma((NY,)),
            dma((NY,)),
            dma((NY,)),
            dma((NY,)),
            dma((NY,)),
            dma((NY,)),
            dma((ACT, NY)),
            dma((ACT, NY)),
            dma((NY,)),
            dma((NY,)),
            dma((ACT, NZ)),
            dma((ACT, NZ)),
            dma((ACT, NY)),
            dma((ACT, NY)),
            dma((5,)),
        ],
        compiler_params=pltpu.CompilerParams(
            collective_id=0, has_side_effects=True, vmem_limit_bytes=56 * 1024 * 1024
        ),
    )(
        particles,
        speeds,
        cell_table,
        top_cells,
        active_ids,
        active_count,
        cell_lists,
        cell_requests[0].T,
        leaf_requests[0].T,
        leaf_lists,
        targets,
    )
    return placed, jnp.transpose(moved, (1, 0, 2))


def solution(mesh):
    placed = (
        P(("leaf", "bulk"), None, None),
        P(("leaf", "bulk"), None, None),
        P(None, ("leaf", "bulk")),
        P(None, "leaf"),
        P(("leaf", "bulk")),
        P(("leaf", "bulk")),
        P(("leaf", "bulk"), None, None),
        P(("leaf", "bulk"), None),
        P(("leaf", "bulk"), None, None),
        P(("leaf", "bulk"), None),
        P(("leaf", "bulk")),
    )
    return jax.shard_map(
        on_device,
        mesh=mesh,
        in_specs=placed,
        out_specs=(P(("leaf", "bulk"), None, None), P(("leaf", "bulk"), None, None)),
        check_vma=False,
    )
```

```python
import functools

import jax
import jax.numpy as jnp
from jax import lax
from jax.experimental import pallas as pl
from jax.experimental.pallas import tpu as pltpu
from jax.sharding import PartitionSpec as P

MESH = pl.DeviceIdType.MESH
step_time = 0.5
pair_soft = 0.01
cell_soft = 1.0

NY, NZ, NL = 4, 16, 8
NB = 32
ACT = 4
LPER = 6
CPER = 64
SUBS = 4
SROW = NB // SUBS
OCT = 64


def pair_terms(px, py, pz, src, accs):
    ax, ay, az = accs
    for sx, sy, sz, sm in src:
        dx = sx - px
        dy = sy - py
        dz = sz - pz
        inv = lax.rsqrt(dx * dx + dy * dy + (dz * dz + pair_soft))
        w = sm * inv * (inv * inv)
        ax = ax + w * dx
        ay = ay + w * dy
        az = az + w * dz
    return ax, ay, az


def cell_terms(px, py, pz, cells, accs):
    ax, ay, az = accs
    for m, cx, cy, cz, xx, yy, zz, xy, xz, yz in cells:
        dx = px - cx
        dy = py - cy
        dz = pz - cz
        inv = lax.rsqrt(dx * dx + dy * dy + (dz * dz + cell_soft))
        inv2 = inv * inv
        inv3 = inv2 * inv
        inv5 = inv3 * inv2
        tx = xx * dx + xy * dy + xz * dz
        ty = xy * dx + yy * dy + yz * dz
        tz = xz * dx + yz * dy + zz * dz
        u = dx * tx + dy * ty + dz * tz
        rad = m * inv3 + (2.5 * u) * (inv5 * inv2)
        ax = ax + (tx * inv5 - rad * dx)
        ay = ay + (ty * inv5 - rad * dy)
        az = az + (tz * inv5 - rad * dz)
    return ax, ay, az


def kernel(
    part, vel, cells, top, act_ids, act_cnt, cell_lists, cell_req, leaf_req, leaf_lists, targets,
    outp, outv,
    p_all, v_all, v_y, c_all, t_all, top_m, codes_v, codes_s, l_send,
    l0, l1, l2, l3, k0, k1, k2, k3, p_rec, pts, acc, own, chosen, picks, near,
    p_ss, p_rs, c_ss, c_rs, v_ss, v_rs, t_ss, t_rs, d_ss, d_rs, vy_ss, vy_rs,
    cy_ss, cy_rs, l_ss, l_rs, pr_ss, pr_rs, kz_ss, kz_rs, ky_ss, ky_rs, loc,
):
    l_rec = (l0, l1, l2, l3)
    k_all = (k0, k1, k2, k3)
    leaf = lax.axis_index("leaf")
    bulk = lax.axis_index("bulk")
    y = bulk // NZ
    z = bulk % NZ

    def row_peer(d):
        return y * NZ + (z + d) % NZ

    def col_peer(d):
        return ((y + d) % NY) * NZ + z

    def ident_of(a):
        return jnp.where(a < act_cnt[0], act_ids[a], -1).astype(jnp.float32)

    own_p = pltpu.make_async_copy(part, p_all.at[z], loc.at[0])
    own_v = pltpu.make_async_copy(vel, v_y.at[pl.ds(y * 3, 3)], loc.at[1])
    own_p.start()
    own_v.start()
    tall = jnp.transpose(
        jnp.concatenate([cells[...], jnp.zeros((128 - 10, 256), jnp.float32)], axis=0)
    )
    packed = tall[0:32]
    for g in range(1, 8):
        packed = packed + pltpu.roll(tall[32 * g : 32 * g + 32], 16 * g, 1)
    c_all[bulk, pl.ds(0, 32), :] = packed
    c_all[bulk, pl.ds(32, 8), :] = jnp.concatenate(
        [jnp.full((1, 128), ident_of(a), jnp.float32) for a in range(ACT)]
        + [jnp.zeros((4, 128), jnp.float32)],
        axis=0,
    )
    t_all[leaf] = jnp.zeros((16, 128), jnp.float32)
    t_all[leaf, pl.ds(0, 10), pl.ds(0, 64)] = top[...]

    def code_of(a, e):
        f = leaf_lists[a, e]
        peer = f // LCAP
        return peer * NB + leaf_req[f % LCAP, peer]

    LCAP = 2
    rows = lax.broadcasted_iota(jnp.int32, (8, 128), 0)
    lanes = lax.broadcasted_iota(jnp.int32, (8, 128), 1)
    code = jnp.zeros((8, 128), jnp.int32)
    for a in range(ACT):
        for e in range(LPER):
            code = jnp.where((rows == a) & (lanes == e), code_of(a, e), code)
    codes_v[y] = code

    barrier = pltpu.get_barrier_semaphore()

    def greet(dev):
        pl.semaphore_signal(barrier, inc=1, device_id=dev, device_id_type=MESH)

    for d in (1, NZ - 1):
        greet({"bulk": row_peer(d)})
    for d in range(1, NY):
        greet({"bulk": col_peer(d)})
    for d in range(1, NL):
        greet({"leaf": (leaf + d) % NL})
    pl.semaphore_wait(barrier, 2 + NY + NL - 2)

    def remote(src, dst, ss, rs, dev):
        return pltpu.make_async_remote_copy(
            src_ref=src, dst_ref=dst, send_sem=ss, recv_sem=rs, device_id=dev, device_id_type=MESH
        )

    def ring_dev(way):
        return {"bulk": row_peer(1 if way == 0 else NZ - 1)}

    def ring_src(way, h):
        return (z + NZ - h) % NZ if way == 0 else (z + h) % NZ

    def p_copy(way, h, sub, first=False):
        at = ring_src(way, h)
        cut = pl.ds(sub * SROW, SROW)
        dst = p_all.at[at, cut]
        src = part.at[cut] if first else dst
        return remote(src, dst, p_ss.at[way, h, sub], p_rs.at[way, h, sub], ring_dev(way))

    def c_copy(way, h):
        at = c_all.at[y * NZ + ring_src(way, h)]
        return remote(at, at, c_ss.at[way, h], c_rs.at[way, h], ring_dev(way))

    def v_copy(way, h, sub):
        at = v_all.at[ring_src(way, h), sub]
        return remote(at, at, v_ss.at[way, h, sub], v_rs.at[way, h, sub], ring_dev(way))

    def t_copy(d):
        return remote(t_all.at[leaf], t_all.at[leaf], t_ss.at[d], t_rs.at[d], {"leaf": (leaf + d) % NL})

    def d_copy(d):
        return remote(
            codes_v.at[y], codes_v.at[y], d_ss.at[d], d_rs.at[d], {"bulk": col_peer(d)}
        )

    def y_gather(ref, size, ss, rs, k):
        half = (size + 1) // 2
        if k < 2:
            cut = ref.at[pl.ds(y * size, size)]
        elif k == 2:
            cut = ref.at[pl.ds(((y + NY - 1) % NY) * size, half)]
        else:
            cut = ref.at[pl.ds(((y + 1) % NY) * size + half, size - half)]
        return remote(cut, cut, ss, rs, {"bulk": col_peer(1 if k % 2 == 0 else NY - 1)})

    def vy_copy(k):
        return y_gather(v_y, 3, vy_ss.at[k], vy_rs.at[k], k)

    def cy_copy(k):
        return y_gather(c_all, NZ, cy_ss.at[k], cy_rs.at[k], k)

    def l_copy(a, d):
        return remote(
            l_send.at[d - 1, a], l_rec[a].at[y], l_ss.at[a, d], l_rs.at[a, d],
            {"bulk": col_peer(d)},
        )

    def pr_copy(k):
        return y_gather(p_rec, NB, pr_ss.at[k], pr_rs.at[k], k)

    def ky_copy(a, d):
        cut = k_all[a].at[pl.ds(y * NZ, NZ)]
        return remote(cut, cut, ky_ss.at[a, d], ky_rs.at[a, d], {"bulk": col_peer(d)})

    far = (4, 8, 12)
    close = (1, NZ - 1, 2)

    def kz_copy(a, hop, base=0):
        cut = k_all[a].at[y * NZ + (z + NZ - base) % NZ]
        dist = (base + hop) % NZ
        return remote(cut, cut, kz_ss.at[a, dist], kz_rs.at[a, dist], {"bulk": row_peer(hop)})

    def k_far(a):
        for hop in (8, 4, 12):
            kz_copy(a, hop).start()
        for hop in close:
            kz_copy(a, hop).start()

    def k_row(a):
        for hop in range(1, NZ):
            kz_copy(a, (NZ // 2 + hop * (hop % 2 * 2 - 1) // 2) % NZ).start()

    def k_close(a):
        for base in far:
            kz_copy(a, base).wait_recv()
            for hop in close:
                kz_copy(a, hop, base).start()

    def y_send(a):
        for dist in range(1, NZ):
            if a == ACT - 1 or dist not in far:
                kz_copy(a, dist).wait_recv()
        for d in (2, 1, 3):
            ky_copy(a, d).start()

    def y_forward(copy):
        for k in range(2):
            copy(k).wait_recv()
        for k in range(2, 4):
            copy(k).start()

    def y_done(copy):
        for k in range(2, 4):
            copy(k).wait_recv()

    for d in range(1, NL):
        t_copy(d).start()
    for way in range(2):
        c_copy(way, 0).start()
    for d in range(1, NY):
        d_copy(d).start()
    for sub in range(SUBS):
        for way in range(2):
            p_copy(way, 0, sub, True).start()
    own_v.wait()
    for k in range(2):
        vy_copy(k).start()

    for a in range(ACT):
        bucket = part[act_ids[a]]
        own[a, pl.ds(0, 4), :] = bucket

        def spread(c, _, a=a):
            row = own[a, pl.ds(c, 1), :]
            pts[a, c] = jnp.transpose(jnp.broadcast_to(row, (128, 512)))
            return 0

        lax.fori_loop(0, 3, spread, 0)

    for d in range(1, NL):
        t_copy(d).wait_recv()
    half = lax.broadcasted_iota(jnp.int32, (16, 128), 1) < 64
    for i in range(4):
        top_m[:, pl.ds(i * 128, 128)] = jnp.where(
            half, t_all[2 * i], pltpu.roll(t_all[2 * i + 1], 64, 1)
        )

    def src_rows(load, tiles=4):
        out = []
        for i in range(tiles):
            sx, sy, sz, sm = [load(c, pl.ds(i * 128, 128)) for c in range(4)]
            out.append((sx, sy, sz, sm * (1.0 / (512.0 * (LPER + 1)))))
        return out

    def self_top(a, o0, count):
        src = src_rows(lambda c, cut: own[a, pl.ds(c, 1), cut])

        def step(i, _):
            at = pl.ds(pl.multiple_of((o0 + i) * 8, 8), 8)
            px, py, pz = pts[a, 0, at, :], pts[a, 1, at, :], pts[a, 2, at, :]
            zero = jnp.zeros((8, 128), jnp.float32)
            accs = pair_terms(px, py, pz, src, (zero, zero, zero))
            tops = [
                [top_m[pl.ds(k, 1), pl.ds(j * 128, 128)] for k in range(10)] for j in range(4)
            ]
            accs = cell_terms(px, py, pz, tops, accs)
            for c in range(3):
                acc[a, c, at, :] = accs[c]
            return 0

        lax.fori_loop(0, count, step, 0, unroll=2)

    def near_part(a, o0, count):
        cut = pl.ds(pl.multiple_of((a // 2) * 128, 128), 128)
        lane = lax.broadcasted_iota(jnp.int32, (1, 128), 1)
        mine = (lane // CPER) == (a % 2)
        cell = [near[pl.ds(k, 1), cut] for k in range(10)]
        cell = [v if 1 <= k <= 3 else jnp.where(mine, v, 0.0) for k, v in enumerate(cell)]

        def step(i, _):
            at = pl.ds(pl.multiple_of((o0 + i) * 8, 8), 8)
            px, py, pz = pts[a, 0, at, :], pts[a, 1, at, :], pts[a, 2, at, :]
            accs = tuple(acc[a, c, at, :] for c in range(3))
            accs = cell_terms(px, py, pz, [cell], accs)
            for c in range(3):
                acc[a, c, at, :] = accs[c]
            return 0

        lax.fori_loop(0, count, step, 0, unroll=4)

    def p_event(i):
        h = i // SUBS
        sub = i % SUBS
        for way in range(2):
            mine = (sub < SUBS // 2) if way == 0 else (sub >= SUBS // 2)

            @pl.when((h < NZ // 2 - 1) | mine)
            def _():
                p_copy(way, h, sub).wait_recv()

            @pl.when((h < NZ // 2 - 2) | ((h == NZ // 2 - 2) & mine))
            def _():
                p_copy(way, h + 1, sub).start()

    def c_event(i):
        for way in range(2):
            if way == 0:
                c_copy(way, i).wait_recv()

                @pl.when(i < NZ // 2 - 1)
                def _():
                    c_copy(way, i + 1).start()
            else:

                @pl.when(i < NZ // 2 - 1)
                def _():
                    c_copy(way, i).wait_recv()

                @pl.when(i < NZ // 2 - 2)
                def _():
                    c_copy(way, i + 1).start()

    def more_events(i, _):
        p_event(i)

        @pl.when((i % 2 == 1) & (i < 16))
        def _():
            c_event(i // 2)

        self_top(i // 8, (i % 8) * 8, 8)
        return 0

    lax.fori_loop(0, 8, more_events, 0)
    y_forward(vy_copy)
    lax.fori_loop(8, 16, more_events, 0)

    y_done(vy_copy)

    def pick_row(j, _):
        shift = (targets[j] - bulk) & 63
        to_z = (z + shift) & 15
        from_y = ((y * NZ + to_z - shift) & 63) >> 4
        for c in range(3):
            v_all[z, c, pl.ds(j, 1), :] = v_y[from_y * 3 + c, pl.ds(j, 1), :]
        return 0

    lax.fori_loop(0, NB, pick_row, 0, unroll=8)
    for k in range(2):
        cy_copy(k).start()
    lax.fori_loop(16, 24, more_events, 0)

    y_forward(cy_copy)
    lax.fori_loop(24, 32, more_events, 0)

    own_p.wait()
    for d in range(1, NY):
        d_copy(d).wait_recv()
    codes_copy = pltpu.make_async_copy(codes_v, codes_s, loc.at[2])
    codes_copy.start()
    codes_copy.wait()

    for way in range(2):
        for sub in range(3):
            v_copy(way, 0, sub).start()

    def leaf_at(number):
        return p_all[(number >> 5) & 15, number & 31]

    for a in range(ACT):
        for d in range(1, NY):
            to_y = (y + d) % NY

            def fill(e, _, a=a, d=d, to_y=to_y):
                l_send[d - 1, a, e] = leaf_at(codes_s[to_y, a, e])
                return 0

            lax.fori_loop(0, LPER, fill, 0, unroll=True)
            l_copy(a, d).start()

        def fill_own(e, _, a=a):
            l_rec[a][y, e] = leaf_at(code_of(a, e))
            return 0

        lax.fori_loop(0, LPER, fill_own, 0, unroll=True)

    def pick_moved(j, _):
        from_z = (bulk - (targets[j] - bulk)) & 15
        p_rec[y * NB + j] = p_all[from_z, j]
        return 0

    lax.fori_loop(0, NB, pick_moved, 0, unroll=8)
    for k in range(2):
        pr_copy(k).start()

    y_done(cy_copy)

    def pick_cell(i, _):
        f = cell_lists[i // CPER, i % CPER]
        peer = f >> 4
        col = cell_req[f & 15, peer] & 255
        chosen[pl.ds(i, 1), :] = c_all[peer, pl.ds(col & 31, 1), :]
        picks[pl.ds(i, 1), :] = jnp.full((1, 128), col >> 5, jnp.int32)
        return 0

    lax.fori_loop(0, ACT * CPER, pick_cell, 0, unroll=8)
    got = chosen[...]
    group = picks[...]
    one = jnp.where(group == 0, got, 0.0)
    for g in range(1, 8):
        one = jnp.where(group == g, pltpu.roll(got, 128 - 16 * g, 1), one)
    near[...] = jnp.transpose(one)
    for a in range(ACT):
        near_part(a, 0, OCT)

    def v_event(i):
        h = i // 3
        sub = i % 3
        for way in range(2):
            mine = (sub == 0) if way == 0 else (sub > 0)

            @pl.when((h < NZ // 2 - 1) | mine)
            def _():
                v_copy(way, h, sub).wait_recv()

            @pl.when((h < NZ // 2 - 2) | ((h == NZ // 2 - 2) & mine))
            def _():
                v_copy(way, h + 1, sub).start()

    for a in range(ACT):
        for d in range(1, NY):
            l_copy(a, d).wait_recv()
        if a == 3:
            y_forward(pr_copy)

        def block(e, _, a=a):
            from_y = (code_of(a, e) >> 9) & 3
            src = src_rows(lambda c, cut: l_rec[a][from_y, e, pl.ds(c, 1), cut])

            def step(i, _):
                at = pl.ds(pl.multiple_of(i * 8, 8), 8)
                px, py, pz = pts[a, 0, at, :], pts[a, 1, at, :], pts[a, 2, at, :]
                accs = tuple(acc[a, c, at, :] for c in range(3))
                accs = pair_terms(px, py, pz, src, accs)
                for c in range(3):
                    acc[a, c, at, :] = accs[c]
                return 0

            lax.fori_loop(0, OCT, step, 0, unroll=8)

            first = a * 4 - (a > 0)

            @pl.when(e % 2 == 1)
            def _():
                v_event(first + (a > 0) + e // 2)

            if a > 0:

                @pl.when(e == 0)
                def _():
                    v_event(first)

            if a >= 2:

                @pl.when(e == 3)
                def _():
                    k_close(a - 2)

            if a == 3:

                @pl.when(e == 2)
                def _():
                    y_send(0)

            return 0

        lax.fori_loop(0, LPER, block, 0)
        alive = jnp.where(a < act_cnt[0], step_time, 0.0)
        for c in range(3):
            pull = jnp.sum(jnp.transpose(acc[a, c]), axis=0, keepdims=True) * alive
            for b in range(4):
                row, col = divmod(c * 4 + b, 3)
                k_all[a][bulk, pl.ds(row, 1), pl.ds(col * 128, 128)] = pull[
                    :, b * 128 : (b + 1) * 128
                ]
        if a < ACT - 1:
            k_far(a)
        else:
            k_row(a)

    def v_events(lo, hi):
        def go(i, _):
            v_event(i)
            return 0

        lax.fori_loop(lo, hi, go, 0)

    for d in range(1, NL):
        t_copy(d).wait_send()

    def p_sent(i, _):
        h = i // SUBS
        sub = i % SUBS
        for way in range(2):
            mine = (sub < SUBS // 2) if way == 0 else (sub >= SUBS // 2)

            @pl.when((h < NZ // 2 - 1) | mine)
            def _():
                p_copy(way, h, sub).wait_send()

        return 0

    lax.fori_loop(0, 32, p_sent, 0)
    v_events(15, 16)
    y_send(1)
    v_events(16, 17)
    k_close(2)
    v_events(17, 18)
    for h in range(NZ // 2):
        c_copy(0, h).wait_send()
        if h < NZ // 2 - 1:
            c_copy(1, h).wait_send()
    for k in range(4):
        vy_copy(k).wait_send()
        cy_copy(k).wait_send()
    for d in range(1, NY):
        d_copy(d).wait_send()
        for a in range(ACT):
            l_copy(a, d).wait_send()
    v_events(18, 19)
    y_send(2)
    v_events(19, 21)
    y_done(pr_copy)
    for k in range(4):
        pr_copy(k).wait_send()
    y_send(3)
    v_events(21, 24)

    def v_sent(i, _):
        h = i // 3
        sub = i % 3
        for way in range(2):
            mine = (sub == 0) if way == 0 else (sub > 0)

            @pl.when((h < NZ // 2 - 1) | mine)
            def _():
                v_copy(way, h, sub).wait_send()

        return 0

    lax.fori_loop(0, 24, v_sent, 0)
    for a in range(ACT):
        for dist in range(1, NZ):
            kz_copy(a, dist).wait_send()
    for a in range(ACT):
        for d in range(1, NY):
            ky_copy(a, d).wait_recv()

    def place(j, _):
        source = (bulk - (targets[j] - bulk)) & 63
        from_y = source >> 4
        from_z = source & 15
        number = j.astype(jnp.float32)
        hits = [c_all[source, pl.ds(32 + a, 1), :] == number for a in range(ACT)]
        for c in range(3):
            parts = []
            for b in range(4):
                row, col = divmod(c * 4 + b, 3)
                kick = jnp.zeros((1, 128), jnp.float32)
                for a in range(ACT):
                    got = k_all[a][source, pl.ds(row, 1), pl.ds(col * 128, 128)]
                    kick = kick + jnp.where(hits[a], got, 0.0)
                parts.append(kick)
            speed = v_all[from_z, c, pl.ds(j, 1), :] + jnp.concatenate(parts, axis=1)
            outv[c, pl.ds(j, 1), :] = speed
            outp[j, pl.ds(c, 1), :] = p_rec[from_y * NB + j, pl.ds(c, 1), :] + step_time * speed
        outp[j, pl.ds(3, 1), :] = p_rec[from_y * NB + j, pl.ds(3, 1), :]
        return 0

    lax.fori_loop(0, NB, place, 0, unroll=4)

    for a in range(ACT):
        for d in range(1, NY):
            ky_copy(a, d).wait_send()


def on_device(
    particles,
    velocities,
    cell_table,
    top_cells,
    active_ids,
    active_count,
    cell_requests,
    cell_lists,
    leaf_requests,
    leaf_lists,
    targets,
):
    speeds = jnp.transpose(velocities, (1, 0, 2))
    vmem = pl.BlockSpec(memory_space=pltpu.VMEM)
    smem = pl.BlockSpec(memory_space=pltpu.SMEM)
    f32 = jnp.float32
    dma = pltpu.SemaphoreType.DMA
    placed, moved = pl.pallas_call(
        kernel,
        out_shape=(
            jax.ShapeDtypeStruct((NB, 4, 512), f32),
            jax.ShapeDtypeStruct((3, NB, 512), f32),
        ),
        in_specs=[vmem] * 4 + [smem] * 7,
        out_specs=(vmem, vmem),
        scratch_shapes=[
            pltpu.VMEM((NZ, NB, 4, 512), f32),
            pltpu.VMEM((NZ, 3, NB, 512), f32),
            pltpu.VMEM((NY * 3, NB, 512), f32),
            pltpu.VMEM((NY * NZ, 40, 128), f32),
            pltpu.VMEM((NL, 16, 128), f32),
            pltpu.VMEM((16, 512), f32),
            pltpu.VMEM((NY, 8, 128), jnp.int32),
            pltpu.SMEM((NY, 8, 128), jnp.int32),
            pltpu.VMEM((NY - 1, ACT, LPER, 4, 512), f32),
        ]
        + [pltpu.VMEM((NY, LPER, 4, 512), f32)] * ACT
        + [pltpu.VMEM((NY * NZ, 4, 384), f32)] * ACT
        + [
            pltpu.VMEM((NY * NB, 4, 512), f32),
            pltpu.VMEM((ACT, 3, 512, 128), f32),
            pltpu.VMEM((ACT, 3, 512, 128), f32),
            pltpu.VMEM((ACT, 8, 512), f32),
            pltpu.VMEM((ACT * CPER, 128), f32),
            pltpu.VMEM((ACT * CPER, 128), jnp.int32),
            pltpu.VMEM((128, ACT * CPER), f32),
            dma((2, 8, SUBS)),
            dma((2, 8, SUBS)),
            dma((2, 8)),
            dma((2, 8)),
            dma((2, 8, 3)),
            dma((2, 8, 3)),
            dma((NL,)),
            dma((NL,)),
            dma((NY,)),
            dma((NY,)),
            dma((NY,)),
            dma((NY,)),
            dma((NY,)),
            dma((NY,)),
            dma((ACT, NY)),
            dma((ACT, NY)),
            dma((NY,)),
            dma((NY,)),
            dma((ACT, NZ)),
            dma((ACT, NZ)),
            dma((ACT, NY)),
            dma((ACT, NY)),
            dma((5,)),
        ],
        compiler_params=pltpu.CompilerParams(
            collective_id=0, has_side_effects=True, vmem_limit_bytes=56 * 1024 * 1024
        ),
    )(
        particles,
        speeds,
        cell_table,
        top_cells,
        active_ids,
        active_count,
        cell_lists,
        cell_requests[0].T,
        leaf_requests[0].T,
        leaf_lists,
        targets,
    )
    return placed, jnp.transpose(moved, (1, 0, 2))


def solution(mesh):
    placed = (
        P(("leaf", "bulk"), None, None),
        P(("leaf", "bulk"), None, None),
        P(None, ("leaf", "bulk")),
        P(None, "leaf"),
        P(("leaf", "bulk")),
        P(("leaf", "bulk")),
        P(("leaf", "bulk"), None, None),
        P(("leaf", "bulk"), None),
        P(("leaf", "bulk"), None, None),
        P(("leaf", "bulk"), None),
        P(("leaf", "bulk")),
    )
    return jax.shard_map(
        on_device,
        mesh=mesh,
        in_specs=placed,
        out_specs=(P(("leaf", "bulk"), None, None), P(("leaf", "bulk"), None, None)),
        check_vma=False,
    )
```

```python
import functools

import jax
import jax.numpy as jnp
from jax import lax
from jax.experimental import pallas as pl
from jax.experimental.pallas import tpu as pltpu
from jax.sharding import PartitionSpec as P

MESH = pl.DeviceIdType.MESH
step_time = 0.5
pair_soft = 0.01
cell_soft = 1.0

NY, NZ, NL = 4, 16, 8
NB = 32
ACT = 4
LPER = 6
CPER = 64
SUBS = 4
SROW = NB // SUBS
OCT = 64
V_CAP = [NB] + [min(NB - 2, 8 * (8 - h) + 4) for h in range(1, 9)]
V_PLAN = (
    ((1, 0), (3, 1), (5, 2)),
    ((0, 3), (1, 4), (3, 5), (5, 6)),
    ((0, 7), (1, 8), (3, 9), (5, 10)),
    ((0, 11), (1, 12), (3, 13), (5, 14)),
)


def pair_terms(px, py, pz, src, accs):
    ax, ay, az = accs
    for sx, sy, sz, sm in src:
        dx = sx - px
        dy = sy - py
        dz = sz - pz
        inv = lax.rsqrt(dx * dx + dy * dy + (dz * dz + pair_soft))
        w = sm * inv * (inv * inv)
        ax = ax + w * dx
        ay = ay + w * dy
        az = az + w * dz
    return ax, ay, az


def cell_terms(px, py, pz, cells, accs):
    ax, ay, az = accs
    for m, cx, cy, cz, xx, yy, zz, xy, xz, yz in cells:
        dx = px - cx
        dy = py - cy
        dz = pz - cz
        inv = lax.rsqrt(dx * dx + dy * dy + (dz * dz + cell_soft))
        inv2 = inv * inv
        inv3 = inv2 * inv
        inv5 = inv3 * inv2
        tx = xx * dx + xy * dy + xz * dz
        ty = xy * dx + yy * dy + yz * dz
        tz = xz * dx + yz * dy + zz * dz
        u = dx * tx + dy * ty + dz * tz
        rad = m * inv3 + (2.5 * u) * (inv5 * inv2)
        ax = ax + (tx * inv5 - rad * dx)
        ay = ay + (ty * inv5 - rad * dy)
        az = az + (tz * inv5 - rad * dz)
    return ax, ay, az


def kernel(
    part, vel, cells, top, act_ids, act_cnt, cell_lists, cell_req, leaf_req, leaf_lists, targets,
    outp, outv,
    p_all, v_rg, tab_v, tab_s, v_y, c_all, t_all, top_m, codes_v, codes_s, l_send,
    l0, l1, l2, l3, k0, k1, k2, k3, p_rec, pts, acc, own, chosen, picks, near,
    p_ss, p_rs, c_ss, c_rs, v_ss, v_rs, t_ss, t_rs, d_ss, d_rs, vy_ss, vy_rs,
    cy_ss, cy_rs, l_ss, l_rs, pr_ss, pr_rs, kz_ss, kz_rs, ky_ss, ky_rs, loc,
):
    l_rec = (l0, l1, l2, l3)
    k_all = (k0, k1, k2, k3)
    leaf = lax.axis_index("leaf")
    bulk = lax.axis_index("bulk")
    y = bulk // NZ
    z = bulk % NZ

    def row_peer(d):
        return y * NZ + (z + d) % NZ

    def col_peer(d):
        return ((y + d) % NY) * NZ + z

    def ident_of(a):
        return jnp.where(a < act_cnt[0], act_ids[a], -1).astype(jnp.float32)

    own_p = pltpu.make_async_copy(part, p_all.at[z], loc.at[0])
    own_v = pltpu.make_async_copy(vel, v_y.at[pl.ds(y * 3, 3)], loc.at[1])
    own_p.start()
    own_v.start()
    tall = jnp.transpose(
        jnp.concatenate([cells[...], jnp.zeros((128 - 10, 256), jnp.float32)], axis=0)
    )
    packed = tall[0:32]
    for g in range(1, 8):
        packed = packed + pltpu.roll(tall[32 * g : 32 * g + 32], 16 * g, 1)
    c_all[bulk, pl.ds(0, 32), :] = packed
    c_all[bulk, pl.ds(32, 8), :] = jnp.concatenate(
        [jnp.full((1, 128), ident_of(a), jnp.float32) for a in range(ACT)]
        + [jnp.zeros((4, 128), jnp.float32)],
        axis=0,
    )
    t_all[leaf] = jnp.zeros((16, 128), jnp.float32)
    t_all[leaf, pl.ds(0, 10), pl.ds(0, 64)] = top[...]

    def code_of(a, e):
        f = leaf_lists[a, e]
        peer = f // LCAP
        return peer * NB + leaf_req[f % LCAP, peer]

    LCAP = 2
    rows = lax.broadcasted_iota(jnp.int32, (8, 128), 0)
    lanes = lax.broadcasted_iota(jnp.int32, (8, 128), 1)
    code = jnp.zeros((8, 128), jnp.int32)
    for a in range(ACT):
        for e in range(LPER):
            code = jnp.where((rows == a) & (lanes == e), code_of(a, e), code)
    codes_v[y] = code

    barrier = pltpu.get_barrier_semaphore()

    def greet(dev):
        pl.semaphore_signal(barrier, inc=1, device_id=dev, device_id_type=MESH)

    for d in (1, NZ - 1):
        greet({"bulk": row_peer(d)})
    for d in range(1, NY):
        greet({"bulk": col_peer(d)})
    for d in range(1, NL):
        greet({"leaf": (leaf + d) % NL})
    pl.semaphore_wait(barrier, 2 + NY + NL - 2)

    def remote(src, dst, ss, rs, dev):
        return pltpu.make_async_remote_copy(
            src_ref=src, dst_ref=dst, send_sem=ss, recv_sem=rs, device_id=dev, device_id_type=MESH
        )

    def ring_dev(way):
        return {"bulk": row_peer(1 if way == 0 else NZ - 1)}

    def ring_src(way, h):
        return (z + NZ - h) % NZ if way == 0 else (z + h) % NZ

    def p_copy(way, h, sub, first=False):
        at = ring_src(way, h)
        cut = pl.ds(sub * SROW, SROW)
        dst = p_all.at[at, cut]
        src = part.at[cut] if first else dst
        return remote(src, dst, p_ss.at[way, h, sub], p_rs.at[way, h, sub], ring_dev(way))

    def c_copy(way, h):
        at = c_all.at[y * NZ + ring_src(way, h)]
        return remote(at, at, c_ss.at[way, h], c_rs.at[way, h], ring_dev(way))

    def v_cut(h, sub):
        lo, hi = sub * 10, min(sub * 10 + 10, V_CAP[h])
        return lo, hi - lo

    def v_copy(way, h, sub):
        lo, size = v_cut(h, sub)
        src = v_rg.at[pl.ds((way * 9 + h - 1) * NB + lo, size)]
        dst = v_rg.at[pl.ds((way * 9 + h) * NB + lo, size)]
        return remote(src, dst, v_ss.at[way, h, sub], v_rs.at[way, h, sub], ring_dev(way))

    def t_copy(d):
        return remote(t_all.at[leaf], t_all.at[leaf], t_ss.at[d], t_rs.at[d], {"leaf": (leaf + d) % NL})

    def d_copy(d):
        return remote(
            codes_v.at[y], codes_v.at[y], d_ss.at[d], d_rs.at[d], {"bulk": col_peer(d)}
        )

    def y_gather(ref, size, ss, rs, k):
        half = (size + 1) // 2
        if k < 2:
            cut = ref.at[pl.ds(y * size, size)]
        elif k == 2:
            cut = ref.at[pl.ds(((y + NY - 1) % NY) * size, half)]
        else:
            cut = ref.at[pl.ds(((y + 1) % NY) * size + half, size - half)]
        return remote(cut, cut, ss, rs, {"bulk": col_peer(1 if k % 2 == 0 else NY - 1)})

    def vy_copy(k):
        return y_gather(v_y, 3, vy_ss.at[k], vy_rs.at[k], k)

    def cy_copy(k):
        return y_gather(c_all, NZ, cy_ss.at[k], cy_rs.at[k], k)

    def l_copy(a, d):
        return remote(
            l_send.at[d - 1, a], l_rec[a].at[y], l_ss.at[a, d], l_rs.at[a, d],
            {"bulk": col_peer(d)},
        )

    def pr_copy(k):
        return y_gather(p_rec, NB, pr_ss.at[k], pr_rs.at[k], k)

    def ky_copy(a, d):
        cut = k_all[a].at[pl.ds(y * NZ, NZ)]
        return remote(cut, cut, ky_ss.at[a, d], ky_rs.at[a, d], {"bulk": col_peer(d)})

    far = (4, 8, 12)
    close = (1, NZ - 1, 2)

    def kz_copy(a, hop, base=0):
        cut = k_all[a].at[y * NZ + (z + NZ - base) % NZ]
        dist = (base + hop) % NZ
        return remote(cut, cut, kz_ss.at[a, dist], kz_rs.at[a, dist], {"bulk": row_peer(hop)})

    def k_far(a):
        for hop in (8, 4, 12):
            kz_copy(a, hop).start()
        for hop in close:
            kz_copy(a, hop).start()

    def k_row(a):
        for hop in range(1, NZ):
            kz_copy(a, (NZ // 2 + hop * (hop % 2 * 2 - 1) // 2) % NZ).start()

    def k_close(a):
        for base in far:
            kz_copy(a, base).wait_recv()
            for hop in close:
                kz_copy(a, hop, base).start()

    def y_send(a):
        for dist in range(1, NZ):
            if a == ACT - 1 or dist not in far:
                kz_copy(a, dist).wait_recv()
        for d in (2, 1, 3):
            ky_copy(a, d).start()

    def y_forward(copy):
        for k in range(2):
            copy(k).wait_recv()
        for k in range(2, 4):
            copy(k).start()

    def y_done(copy):
        for k in range(2, 4):
            copy(k).wait_recv()

    for d in range(1, NL):
        t_copy(d).start()
    for way in range(2):
        c_copy(way, 0).start()
    for d in range(1, NY):
        d_copy(d).start()
    for sub in range(SUBS):
        for way in range(2):
            p_copy(way, 0, sub, True).start()
    own_v.wait()
    for k in range(2):
        vy_copy(k).start()

    row32 = lax.broadcasted_iota(jnp.int32, (32, 128), 0)
    offs = [(targets[j] - bulk) & 15 for j in range(NB)]
    off_col = jnp.zeros((32, 128), jnp.int32)
    off_row = jnp.zeros((8, 128), jnp.int32)
    for j in range(NB):
        off_col = jnp.where(row32 == j, offs[j], off_col)
        off_row = jnp.where(lanes == j, offs[j], off_row)
    half_col = jnp.zeros((32, 128), jnp.int32)
    half_row = jnp.zeros((8, 128), jnp.int32)
    for j in range(NB):
        half_col = half_col + jnp.where((offs[j] == 8) & (row32 > j), 1, 0)
        half_row = half_row + jnp.where((offs[j] == 8) & (lanes > j), 1, 0)

    def split(off, half):
        back = (off > 8) | ((off == 8) & (half >= 4))
        return jnp.where(back, 0, off), jnp.where(back, 16 - off, 0)

    dist_col = split(off_col, half_col)
    dist_row = split(off_row, half_row)
    table = jnp.zeros((8, 128), jnp.int32)
    code = jnp.zeros((8, 128), jnp.int32)
    for way in range(2):
        place_col = jnp.zeros((32, 128), jnp.int32)
        place_row = jnp.zeros((8, 128), jnp.int32)
        for j in range(NB):
            mine = dist_col[way][j : j + 1, :]
            place_col = place_col + jnp.where(
                (mine > dist_col[way]) | ((mine == dist_col[way]) & (row32 > j)), 1, 0
            )
            place_row = place_row + jnp.where(
                (mine > dist_row[way]) | ((mine == dist_row[way]) & (lanes > j)), 1, 0
            )
        held = jnp.zeros((8, 128), jnp.int32)
        for j in range(NB):
            held = jnp.where(place_col[j : j + 1, :] == lanes, j, held)
        table = jnp.where(rows == way, held, table)
        spot = (way * 9 + dist_row[way]) * NB + place_row
        code = spot if way == 0 else jnp.where(dist_row[1] > 0, spot, code)
    tab_v[...] = jnp.where(rows == 2, code, table)
    tab_copy = pltpu.make_async_copy(tab_v, tab_s, loc.at[3])
    tab_copy.start()

    for a in range(ACT):
        bucket = part[act_ids[a]]
        own[a, pl.ds(0, 4), :] = bucket

        def spread(c, _, a=a):
            row = own[a, pl.ds(c, 1), :]
            pts[a, c] = jnp.transpose(jnp.broadcast_to(row, (128, 512)))
            return 0

        lax.fori_loop(0, 3, spread, 0)

    for d in range(1, NL):
        t_copy(d).wait_recv()
    half = lax.broadcasted_iota(jnp.int32, (16, 128), 1) < 64
    for i in range(4):
        top_m[:, pl.ds(i * 128, 128)] = jnp.where(
            half, t_all[2 * i], pltpu.roll(t_all[2 * i + 1], 64, 1)
        )

    def src_rows(load, tiles=4):
        out = []
        for i in range(tiles):
            sx, sy, sz, sm = [load(c, pl.ds(i * 128, 128)) for c in range(4)]
            out.append((sx, sy, sz, sm * (1.0 / (512.0 * (LPER + 1)))))
        return out

    def self_top(a, o0, count):
        src = src_rows(lambda c, cut: own[a, pl.ds(c, 1), cut])

        def step(i, _):
            at = pl.ds(pl.multiple_of((o0 + i) * 8, 8), 8)
            px, py, pz = pts[a, 0, at, :], pts[a, 1, at, :], pts[a, 2, at, :]
            zero = jnp.zeros((8, 128), jnp.float32)
            accs = pair_terms(px, py, pz, src, (zero, zero, zero))
            tops = [
                [top_m[pl.ds(k, 1), pl.ds(j * 128, 128)] for k in range(10)] for j in range(4)
            ]
            accs = cell_terms(px, py, pz, tops, accs)
            for c in range(3):
                acc[a, c, at, :] = accs[c]
            return 0

        lax.fori_loop(0, count, step, 0, unroll=2)

    def near_part(a, o0, count):
        cut = pl.ds(pl.multiple_of((a // 2) * 128, 128), 128)
        lane = lax.broadcasted_iota(jnp.int32, (1, 128), 1)
        mine = (lane // CPER) == (a % 2)
        cell = [near[pl.ds(k, 1), cut] for k in range(10)]
        cell = [v if 1 <= k <= 3 else jnp.where(mine, v, 0.0) for k, v in enumerate(cell)]

        def step(i, _):
            at = pl.ds(pl.multiple_of((o0 + i) * 8, 8), 8)
            px, py, pz = pts[a, 0, at, :], pts[a, 1, at, :], pts[a, 2, at, :]
            accs = tuple(acc[a, c, at, :] for c in range(3))
            accs = cell_terms(px, py, pz, [cell], accs)
            for c in range(3):
                acc[a, c, at, :] = accs[c]
            return 0

        lax.fori_loop(0, count, step, 0, unroll=4)

    def p_event(i):
        h = i // SUBS
        sub = i % SUBS
        for way in range(2):
            mine = (sub < SUBS // 2) if way == 0 else (sub >= SUBS // 2)

            @pl.when((h < NZ // 2 - 1) | mine)
            def _():
                p_copy(way, h, sub).wait_recv()

            @pl.when((h < NZ // 2 - 2) | ((h == NZ // 2 - 2) & mine))
            def _():
                p_copy(way, h + 1, sub).start()

    def c_event(i):
        for way in range(2):
            if way == 0:
                c_copy(way, i).wait_recv()

                @pl.when(i < NZ // 2 - 1)
                def _():
                    c_copy(way, i + 1).start()
            else:

                @pl.when(i < NZ // 2 - 1)
                def _():
                    c_copy(way, i).wait_recv()

                @pl.when(i < NZ // 2 - 2)
                def _():
                    c_copy(way, i + 1).start()

    def more_events(i, _):
        p_event(i)

        @pl.when((i % 2 == 1) & (i < 16))
        def _():
            c_event(i // 2)

        self_top(i // 8, (i % 8) * 8, 8)
        return 0

    lax.fori_loop(0, 8, more_events, 0)
    y_forward(vy_copy)
    lax.fori_loop(8, 16, more_events, 0)

    y_done(vy_copy)

    tab_copy.wait()
    for way in range(2):

        def pick_row(slot, _, way=way):
            j = tab_s[way, slot] & 31
            shift = (targets[j] - bulk) & 63
            to_z = (z + shift) & 15
            from_y = ((y * NZ + to_z - shift) & 63) >> 4
            for c in range(3):
                line = v_y[from_y * 3 + c, pl.ds(j, 1), :]
                for b in range(4):
                    row, col = divmod(c * 4 + b, 3)
                    v_rg[way * 9 * NB + slot, pl.ds(row, 1), pl.ds(col * 128, 128)] = line[
                        :, b * 128 : (b + 1) * 128
                    ]
            return 0

        lax.fori_loop(0, NB, pick_row, 0, unroll=4)
    for k in range(2):
        cy_copy(k).start()
    lax.fori_loop(16, 24, more_events, 0)

    y_forward(cy_copy)
    lax.fori_loop(24, 32, more_events, 0)

    own_p.wait()
    for d in range(1, NY):
        d_copy(d).wait_recv()
    codes_copy = pltpu.make_async_copy(codes_v, codes_s, loc.at[2])
    codes_copy.start()
    codes_copy.wait()

    for way in range(2):
        for sub in range(3):
            v_copy(way, 1, sub).start()

    def leaf_at(number):
        return p_all[(number >> 5) & 15, number & 31]

    for a in range(ACT):
        for d in range(1, NY):
            to_y = (y + d) % NY

            def fill(e, _, a=a, d=d, to_y=to_y):
                l_send[d - 1, a, e] = leaf_at(codes_s[to_y, a, e])
                return 0

            lax.fori_loop(0, LPER, fill, 0, unroll=True)
            l_copy(a, d).start()

        def fill_own(e, _, a=a):
            l_rec[a][y, e] = leaf_at(code_of(a, e))
            return 0

        lax.fori_loop(0, LPER, fill_own, 0, unroll=True)

    def pick_moved(j, _):
        from_z = (bulk - (targets[j] - bulk)) & 15
        p_rec[y * NB + j] = p_all[from_z, j]
        return 0

    lax.fori_loop(0, NB, pick_moved, 0, unroll=8)
    for k in range(2):
        pr_copy(k).start()

    y_done(cy_copy)

    def pick_cell(i, _):
        f = cell_lists[i // CPER, i % CPER]
        peer = f >> 4
        col = cell_req[f & 15, peer] & 255
        chosen[pl.ds(i, 1), :] = c_all[peer, pl.ds(col & 31, 1), :]
        picks[pl.ds(i, 1), :] = jnp.full((1, 128), col >> 5, jnp.int32)
        return 0

    lax.fori_loop(0, ACT * CPER, pick_cell, 0, unroll=8)
    got = chosen[...]
    group = picks[...]
    one = jnp.where(group == 0, got, 0.0)
    for g in range(1, 8):
        one = jnp.where(group == g, pltpu.roll(got, 128 - 16 * g, 1), one)
    near[...] = jnp.transpose(one)
    for a in range(ACT):
        near_part(a, 0, OCT)

    hops = [(h, sub) for h in range(1, 9) for sub in range(3) if V_CAP[h] > sub * 10]

    def v_event(i):
        h, sub = hops[i]
        for way in range(2):
            v_copy(way, h, sub).wait_recv()
            if (h + 1, sub) in hops:
                v_copy(way, h + 1, sub).start()

    def v_events(lo, hi):
        for i in range(lo, hi):
            v_event(i)

    for a in range(ACT):
        for d in range(1, NY):
            l_copy(a, d).wait_recv()
        if a == 3:
            y_forward(pr_copy)

        def block(e, _, a=a):
            from_y = (code_of(a, e) >> 9) & 3
            src = src_rows(lambda c, cut: l_rec[a][from_y, e, pl.ds(c, 1), cut])

            def step(i, _):
                at = pl.ds(pl.multiple_of(i * 8, 8), 8)
                px, py, pz = pts[a, 0, at, :], pts[a, 1, at, :], pts[a, 2, at, :]
                accs = tuple(acc[a, c, at, :] for c in range(3))
                accs = pair_terms(px, py, pz, src, accs)
                for c in range(3):
                    acc[a, c, at, :] = accs[c]
                return 0

            lax.fori_loop(0, OCT, step, 0, unroll=8)

            for at, number in V_PLAN[a]:

                @pl.when(e == at)
                def _(number=number):
                    v_event(number)

            if a >= 2:

                @pl.when(e == 3)
                def _():
                    k_close(a - 2)

            if a == 3:

                @pl.when(e == 2)
                def _():
                    y_send(0)

            return 0

        lax.fori_loop(0, LPER, block, 0)
        alive = jnp.where(a < act_cnt[0], step_time, 0.0)
        for c in range(3):
            pull = jnp.sum(jnp.transpose(acc[a, c]), axis=0, keepdims=True) * alive
            for b in range(4):
                row, col = divmod(c * 4 + b, 3)
                k_all[a][bulk, pl.ds(row, 1), pl.ds(col * 128, 128)] = pull[
                    :, b * 128 : (b + 1) * 128
                ]
        if a < ACT - 1:
            k_far(a)
        else:
            k_row(a)

    for d in range(1, NL):
        t_copy(d).wait_send()

    def p_sent(i, _):
        h = i // SUBS
        sub = i % SUBS
        for way in range(2):
            mine = (sub < SUBS // 2) if way == 0 else (sub >= SUBS // 2)

            @pl.when((h < NZ // 2 - 1) | mine)
            def _():
                p_copy(way, h, sub).wait_send()

        return 0

    lax.fori_loop(0, 32, p_sent, 0)
    y_send(1)
    v_events(15, 16)
    k_close(2)
    v_events(16, 17)
    for h in range(NZ // 2):
        c_copy(0, h).wait_send()
        if h < NZ // 2 - 1:
            c_copy(1, h).wait_send()
    for k in range(4):
        vy_copy(k).wait_send()
        cy_copy(k).wait_send()
    for d in range(1, NY):
        d_copy(d).wait_send()
        for a in range(ACT):
            l_copy(a, d).wait_send()
    y_send(2)
    v_events(17, 18)
    y_done(pr_copy)
    for k in range(4):
        pr_copy(k).wait_send()
    y_send(3)
    v_events(18, 20)
    for h, sub in hops:
        for way in range(2):
            v_copy(way, h, sub).wait_send()
    for a in range(ACT):
        for dist in range(1, NZ):
            kz_copy(a, dist).wait_send()
    for a in range(ACT):
        for d in range(1, NY):
            ky_copy(a, d).wait_recv()

    def place(j, _):
        source = (bulk - (targets[j] - bulk)) & 63
        from_y = source >> 4
        spot_j = tab_s[2, j]
        number = j.astype(jnp.float32)
        hits = [c_all[source, pl.ds(32 + a, 1), :] == number for a in range(ACT)]
        for c in range(3):
            parts = []
            for b in range(4):
                row, col = divmod(c * 4 + b, 3)
                cut = pl.ds(col * 128, 128)
                kick = jnp.zeros((1, 128), jnp.float32)
                for a in range(ACT):
                    got = k_all[a][source, pl.ds(row, 1), cut]
                    kick = kick + jnp.where(hits[a], got, 0.0)
                parts.append(v_rg[spot_j, pl.ds(row, 1), cut] + kick)
            speed = jnp.concatenate(parts, axis=1)
            outv[c, pl.ds(j, 1), :] = speed
            outp[j, pl.ds(c, 1), :] = p_rec[from_y * NB + j, pl.ds(c, 1), :] + step_time * speed
        outp[j, pl.ds(3, 1), :] = p_rec[from_y * NB + j, pl.ds(3, 1), :]
        return 0

    lax.fori_loop(0, NB, place, 0, unroll=4)

    for a in range(ACT):
        for d in range(1, NY):
            ky_copy(a, d).wait_send()


def on_device(
    particles,
    velocities,
    cell_table,
    top_cells,
    active_ids,
    active_count,
    cell_requests,
    cell_lists,
    leaf_requests,
    leaf_lists,
    targets,
):
    speeds = jnp.transpose(velocities, (1, 0, 2))
    vmem = pl.BlockSpec(memory_space=pltpu.VMEM)
    smem = pl.BlockSpec(memory_space=pltpu.SMEM)
    f32 = jnp.float32
    dma = pltpu.SemaphoreType.DMA
    placed, moved = pl.pallas_call(
        kernel,
        out_shape=(
            jax.ShapeDtypeStruct((NB, 4, 512), f32),
            jax.ShapeDtypeStruct((3, NB, 512), f32),
        ),
        in_specs=[vmem] * 4 + [smem] * 7,
        out_specs=(vmem, vmem),
        scratch_shapes=[
            pltpu.VMEM((NZ, NB, 4, 512), f32),
            pltpu.VMEM((2 * 9 * NB, 4, 384), f32),
            pltpu.VMEM((8, 128), jnp.int32),
            pltpu.SMEM((8, 128), jnp.int32),
            pltpu.VMEM((NY * 3, NB, 512), f32),
            pltpu.VMEM((NY * NZ, 40, 128), f32),
            pltpu.VMEM((NL, 16, 128), f32),
            pltpu.VMEM((16, 512), f32),
            pltpu.VMEM((NY, 8, 128), jnp.int32),
            pltpu.SMEM((NY, 8, 128), jnp.int32),
            pltpu.VMEM((NY - 1, ACT, LPER, 4, 512), f32),
        ]
        + [pltpu.VMEM((NY, LPER, 4, 512), f32)] * ACT
        + [pltpu.VMEM((NY * NZ, 4, 384), f32)] * ACT
        + [
            pltpu.VMEM((NY * NB, 4, 512), f32),
            pltpu.VMEM((ACT, 3, 512, 128), f32),
            pltpu.VMEM((ACT, 3, 512, 128), f32),
            pltpu.VMEM((ACT, 8, 512), f32),
            pltpu.VMEM((ACT * CPER, 128), f32),
            pltpu.VMEM((ACT * CPER, 128), jnp.int32),
            pltpu.VMEM((128, ACT * CPER), f32),
            dma((2, 8, SUBS)),
            dma((2, 8, SUBS)),
            dma((2, 8)),
            dma((2, 8)),
            dma((2, 9, 3)),
            dma((2, 9, 3)),
            dma((NL,)),
            dma((NL,)),
            dma((NY,)),
            dma((NY,)),
            dma((NY,)),
            dma((NY,)),
            dma((NY,)),
            dma((NY,)),
            dma((ACT, NY)),
            dma((ACT, NY)),
            dma((NY,)),
            dma((NY,)),
            dma((ACT, NZ)),
            dma((ACT, NZ)),
            dma((ACT, NY)),
            dma((ACT, NY)),
            dma((5,)),
        ],
        compiler_params=pltpu.CompilerParams(
            collective_id=0, has_side_effects=True, vmem_limit_bytes=56 * 1024 * 1024
        ),
    )(
        particles,
        speeds,
        cell_table,
        top_cells,
        active_ids,
        active_count,
        cell_lists,
        cell_requests[0].T,
        leaf_requests[0].T,
        leaf_lists,
        targets,
    )
    return placed, jnp.transpose(moved, (1, 0, 2))


def solution(mesh):
    placed = (
        P(("leaf", "bulk"), None, None),
        P(("leaf", "bulk"), None, None),
        P(None, ("leaf", "bulk")),
        P(None, "leaf"),
        P(("leaf", "bulk")),
        P(("leaf", "bulk")),
        P(("leaf", "bulk"), None, None),
        P(("leaf", "bulk"), None),
        P(("leaf", "bulk"), None, None),
        P(("leaf", "bulk"), None),
        P(("leaf", "bulk")),
    )
    return jax.shard_map(
        on_device,
        mesh=mesh,
        in_specs=placed,
        out_specs=(P(("leaf", "bulk"), None, None), P(("leaf", "bulk"), None, None)),
        check_vma=False,
    )
```

```python
import functools

import jax
import jax.numpy as jnp
from jax import lax
from jax.experimental import pallas as pl
from jax.experimental.pallas import tpu as pltpu
from jax.sharding import PartitionSpec as P

MESH = pl.DeviceIdType.MESH
step_time = 0.5
pair_soft = 0.01
cell_soft = 1.0

NY, NZ, NL = 4, 16, 8
NB = 32
ACT = 4
LPER = 6
CPER = 64
SUBS = 4
SROW = NB // SUBS
OCT = 64
V_CAP = [NB] + [min(NB - 2, 8 * (8 - h) + 4) for h in range(1, 9)]
V_PLAN = (
    ((0, 0), (1, 1), (3, 2), (5, 3)),
    ((0, 4), (1, 5), (3, 6), (5, 7)),
    ((0, 8), (1, 9), (3, 10), (5, 11)),
    ((0, 12), (1, 13), (3, 14), (5, 15)),
)


def pair_terms(px, py, pz, src, accs):
    ax, ay, az = accs
    for sx, sy, sz, sm in src:
        dx = sx - px
        dy = sy - py
        dz = sz - pz
        inv = lax.rsqrt(dx * dx + dy * dy + (dz * dz + pair_soft))
        w = sm * inv * (inv * inv)
        ax = ax + w * dx
        ay = ay + w * dy
        az = az + w * dz
    return ax, ay, az


def cell_terms(px, py, pz, cells, accs):
    ax, ay, az = accs
    for m, cx, cy, cz, xx, yy, zz, xy, xz, yz in cells:
        dx = px - cx
        dy = py - cy
        dz = pz - cz
        inv = lax.rsqrt(dx * dx + dy * dy + (dz * dz + cell_soft))
        inv2 = inv * inv
        inv3 = inv2 * inv
        inv5 = inv3 * inv2
        tx = xx * dx + xy * dy + xz * dz
        ty = xy * dx + yy * dy + yz * dz
        tz = xz * dx + yz * dy + zz * dz
        u = dx * tx + dy * ty + dz * tz
        rad = m * inv3 + (2.5 * u) * (inv5 * inv2)
        ax = ax + (tx * inv5 - rad * dx)
        ay = ay + (ty * inv5 - rad * dy)
        az = az + (tz * inv5 - rad * dz)
    return ax, ay, az


def kernel(
    part, vel, cells, top, act_ids, act_cnt, cell_lists, cell_req, leaf_req, leaf_lists, targets,
    outp, outv,
    p_all, v_rg, tab_v, tab_s, v_y, c_all, t_all, top_m, codes_v, codes_s, l_send,
    l0, l1, l2, l3, k0, k1, k2, k3, p_rec, pts, acc, own, chosen, picks, near,
    p_ss, p_rs, c_ss, c_rs, v_ss, v_rs, t_ss, t_rs, d_ss, d_rs, vy_ss, vy_rs,
    cy_ss, cy_rs, l_ss, l_rs, pr_ss, pr_rs, kz_ss, kz_rs, ky_ss, ky_rs, loc,
):
    l_rec = (l0, l1, l2, l3)
    k_all = (k0, k1, k2, k3)
    leaf = lax.axis_index("leaf")
    bulk = lax.axis_index("bulk")
    y = bulk // NZ
    z = bulk % NZ

    def row_peer(d):
        return y * NZ + (z + d) % NZ

    def col_peer(d):
        return ((y + d) % NY) * NZ + z

    def ident_of(a):
        return jnp.where(a < act_cnt[0], act_ids[a], -1).astype(jnp.float32)

    own_p = pltpu.make_async_copy(part, p_all.at[z], loc.at[0])
    own_v = pltpu.make_async_copy(vel, v_y.at[pl.ds(y * 3, 3)], loc.at[1])
    own_p.start()
    own_v.start()
    tall = jnp.transpose(
        jnp.concatenate([cells[...], jnp.zeros((128 - 10, 256), jnp.float32)], axis=0)
    )
    packed = tall[0:32]
    for g in range(1, 8):
        packed = packed + pltpu.roll(tall[32 * g : 32 * g + 32], 16 * g, 1)
    c_all[bulk, pl.ds(0, 32), :] = packed
    c_all[bulk, pl.ds(32, 8), :] = jnp.concatenate(
        [jnp.full((1, 128), ident_of(a), jnp.float32) for a in range(ACT)]
        + [jnp.zeros((4, 128), jnp.float32)],
        axis=0,
    )
    t_all[leaf] = jnp.zeros((16, 128), jnp.float32)
    t_all[leaf, pl.ds(0, 10), pl.ds(0, 64)] = top[...]

    def code_of(a, e):
        f = leaf_lists[a, e]
        peer = f // LCAP
        return peer * NB + leaf_req[f % LCAP, peer]

    LCAP = 2
    rows = lax.broadcasted_iota(jnp.int32, (8, 128), 0)
    lanes = lax.broadcasted_iota(jnp.int32, (8, 128), 1)
    code = jnp.zeros((8, 128), jnp.int32)
    for a in range(ACT):
        for e in range(LPER):
            code = jnp.where((rows == a) & (lanes == e), code_of(a, e), code)
    codes_v[y] = code

    barrier = pltpu.get_barrier_semaphore()

    def greet(dev):
        pl.semaphore_signal(barrier, inc=1, device_id=dev, device_id_type=MESH)

    for d in (1, NZ - 1):
        greet({"bulk": row_peer(d)})
    for d in range(1, NY):
        greet({"bulk": col_peer(d)})
    for d in range(1, NL):
        greet({"leaf": (leaf + d) % NL})
    pl.semaphore_wait(barrier, 2 + NY + NL - 2)

    def remote(src, dst, ss, rs, dev):
        return pltpu.make_async_remote_copy(
            src_ref=src, dst_ref=dst, send_sem=ss, recv_sem=rs, device_id=dev, device_id_type=MESH
        )

    def ring_dev(way):
        return {"bulk": row_peer(1 if way == 0 else NZ - 1)}

    def ring_src(way, h):
        return (z + NZ - h) % NZ if way == 0 else (z + h) % NZ

    def p_copy(way, h, sub, first=False):
        at = ring_src(way, h)
        cut = pl.ds(sub * SROW, SROW)
        dst = p_all.at[at, cut]
        src = part.at[cut] if first else dst
        return remote(src, dst, p_ss.at[way, h, sub], p_rs.at[way, h, sub], ring_dev(way))

    def c_copy(way, h):
        at = c_all.at[y * NZ + ring_src(way, h)]
        return remote(at, at, c_ss.at[way, h], c_rs.at[way, h], ring_dev(way))

    def v_cut(h, sub):
        lo, hi = sub * 10, min(sub * 10 + 10, V_CAP[h])
        return lo, hi - lo

    def v_copy(way, h, sub):
        lo, size = v_cut(h, sub)
        src = v_rg.at[pl.ds((way * 9 + h - 1) * NB + lo, size)]
        dst = v_rg.at[pl.ds((way * 9 + h) * NB + lo, size)]
        return remote(src, dst, v_ss.at[way, h, sub], v_rs.at[way, h, sub], ring_dev(way))

    def t_copy(d):
        return remote(t_all.at[leaf], t_all.at[leaf], t_ss.at[d], t_rs.at[d], {"leaf": (leaf + d) % NL})

    def d_copy(d):
        return remote(
            codes_v.at[y], codes_v.at[y], d_ss.at[d], d_rs.at[d], {"bulk": col_peer(d)}
        )

    def y_gather(ref, size, ss, rs, k):
        half = (size + 1) // 2
        if k < 2:
            cut = ref.at[pl.ds(y * size, size)]
        elif k == 2:
            cut = ref.at[pl.ds(((y + NY - 1) % NY) * size, half)]
        else:
            cut = ref.at[pl.ds(((y + 1) % NY) * size + half, size - half)]
        return remote(cut, cut, ss, rs, {"bulk": col_peer(1 if k % 2 == 0 else NY - 1)})

    def vy_copy(k):
        return y_gather(v_y, 3, vy_ss.at[k], vy_rs.at[k], k)

    def cy_copy(k):
        return y_gather(c_all, NZ, cy_ss.at[k], cy_rs.at[k], k)

    def l_copy(a, d):
        return remote(
            l_send.at[d - 1, a], l_rec[a].at[y], l_ss.at[a, d], l_rs.at[a, d],
            {"bulk": col_peer(d)},
        )

    def pr_copy(k):
        return y_gather(p_rec, NB, pr_ss.at[k], pr_rs.at[k], k)

    def ky_copy(a, d):
        cut = k_all[a].at[pl.ds(y * NZ, NZ)]
        return remote(cut, cut, ky_ss.at[a, d], ky_rs.at[a, d], {"bulk": col_peer(d)})

    far = (4, 8, 12)
    close = (1, NZ - 1, 2)

    def kz_copy(a, hop, base=0):
        cut = k_all[a].at[y * NZ + (z + NZ - base) % NZ]
        dist = (base + hop) % NZ
        return remote(cut, cut, kz_ss.at[a, dist], kz_rs.at[a, dist], {"bulk": row_peer(hop)})

    def k_far(a):
        for hop in (8, 4, 12):
            kz_copy(a, hop).start()
        for hop in close:
            kz_copy(a, hop).start()

    def k_row(a):
        for hop in range(1, NZ):
            kz_copy(a, (NZ // 2 + hop * (hop % 2 * 2 - 1) // 2) % NZ).start()

    def k_close(a):
        for base in far:
            kz_copy(a, base).wait_recv()
            for hop in close:
                kz_copy(a, hop, base).start()

    def y_send(a):
        for dist in range(1, NZ):
            if a == ACT - 1 or dist not in far:
                kz_copy(a, dist).wait_recv()
        for d in (2, 1, 3):
            ky_copy(a, d).start()

    def y_forward(copy):
        for k in range(2):
            copy(k).wait_recv()
        for k in range(2, 4):
            copy(k).start()

    def y_done(copy):
        for k in range(2, 4):
            copy(k).wait_recv()

    for d in range(1, NL):
        t_copy(d).start()
    for way in range(2):
        c_copy(way, 0).start()
    for d in range(1, NY):
        d_copy(d).start()
    for sub in range(SUBS):
        for way in range(2):
            p_copy(way, 0, sub, True).start()
    own_v.wait()
    for k in range(2):
        vy_copy(k).start()

    row32 = lax.broadcasted_iota(jnp.int32, (32, 128), 0)
    offs = [(targets[j] - bulk) & 15 for j in range(NB)]
    off_col = jnp.zeros((32, 128), jnp.int32)
    off_row = jnp.zeros((8, 128), jnp.int32)
    for j in range(NB):
        off_col = jnp.where(row32 == j, offs[j], off_col)
        off_row = jnp.where(lanes == j, offs[j], off_row)
    half_col = jnp.zeros((32, 128), jnp.int32)
    half_row = jnp.zeros((8, 128), jnp.int32)
    for j in range(NB):
        half_col = half_col + jnp.where((offs[j] == 8) & (row32 > j), 1, 0)
        half_row = half_row + jnp.where((offs[j] == 8) & (lanes > j), 1, 0)

    def split(off, half):
        back = (off > 8) | ((off == 8) & (half >= 4))
        return jnp.where(back, 0, off), jnp.where(back, 16 - off, 0)

    dist_col = split(off_col, half_col)
    dist_row = split(off_row, half_row)
    table = jnp.zeros((8, 128), jnp.int32)
    code = jnp.zeros((8, 128), jnp.int32)
    for way in range(2):
        place_col = jnp.zeros((32, 128), jnp.int32)
        place_row = jnp.zeros((8, 128), jnp.int32)
        for j in range(NB):
            mine = dist_col[way][j : j + 1, :]
            place_col = place_col + jnp.where(
                (mine > dist_col[way]) | ((mine == dist_col[way]) & (row32 > j)), 1, 0
            )
            place_row = place_row + jnp.where(
                (mine > dist_row[way]) | ((mine == dist_row[way]) & (lanes > j)), 1, 0
            )
        held = jnp.zeros((8, 128), jnp.int32)
        for j in range(NB):
            held = jnp.where(place_col[j : j + 1, :] == lanes, j, held)
        table = jnp.where(rows == way, held, table)
        spot = (way * 9 + dist_row[way]) * NB + place_row
        code = spot if way == 0 else jnp.where(dist_row[1] > 0, spot, code)
    tab_v[...] = jnp.where(rows == 2, code, table)
    tab_copy = pltpu.make_async_copy(tab_v, tab_s, loc.at[3])
    tab_copy.start()

    for a in range(ACT):
        bucket = part[act_ids[a]]
        own[a, pl.ds(0, 4), :] = bucket

        def spread(c, _, a=a):
            row = own[a, pl.ds(c, 1), :]
            pts[a, c] = jnp.transpose(jnp.broadcast_to(row, (128, 512)))
            return 0

        lax.fori_loop(0, 3, spread, 0)

    for d in range(1, NL):
        t_copy(d).wait_recv()
    half = lax.broadcasted_iota(jnp.int32, (16, 128), 1) < 64
    for i in range(4):
        top_m[:, pl.ds(i * 128, 128)] = jnp.where(
            half, t_all[2 * i], pltpu.roll(t_all[2 * i + 1], 64, 1)
        )

    def src_rows(load, tiles=4):
        out = []
        for i in range(tiles):
            sx, sy, sz, sm = [load(c, pl.ds(i * 128, 128)) for c in range(4)]
            out.append((sx, sy, sz, sm * (1.0 / (512.0 * (LPER + 1)))))
        return out

    def self_top(a, o0, count):
        src = src_rows(lambda c, cut: own[a, pl.ds(c, 1), cut])

        def step(i, _):
            at = pl.ds(pl.multiple_of((o0 + i) * 8, 8), 8)
            px, py, pz = pts[a, 0, at, :], pts[a, 1, at, :], pts[a, 2, at, :]
            zero = jnp.zeros((8, 128), jnp.float32)
            accs = pair_terms(px, py, pz, src, (zero, zero, zero))
            tops = [
                [top_m[pl.ds(k, 1), pl.ds(j * 128, 128)] for k in range(10)] for j in range(4)
            ]
            accs = cell_terms(px, py, pz, tops, accs)
            for c in range(3):
                acc[a, c, at, :] = accs[c]
            return 0

        lax.fori_loop(0, count, step, 0, unroll=2)

    def near_part(a, o0, count):
        cut = pl.ds(pl.multiple_of((a // 2) * 128, 128), 128)
        lane = lax.broadcasted_iota(jnp.int32, (1, 128), 1)
        mine = (lane // CPER) == (a % 2)
        cell = [near[pl.ds(k, 1), cut] for k in range(10)]
        cell = [v if 1 <= k <= 3 else jnp.where(mine, v, 0.0) for k, v in enumerate(cell)]

        def step(i, _):
            at = pl.ds(pl.multiple_of((o0 + i) * 8, 8), 8)
            px, py, pz = pts[a, 0, at, :], pts[a, 1, at, :], pts[a, 2, at, :]
            accs = tuple(acc[a, c, at, :] for c in range(3))
            accs = cell_terms(px, py, pz, [cell], accs)
            for c in range(3):
                acc[a, c, at, :] = accs[c]
            return 0

        lax.fori_loop(0, count, step, 0, unroll=4)

    def p_event(i):
        h = i // SUBS
        sub = i % SUBS
        for way in range(2):
            mine = (sub < SUBS // 2) if way == 0 else (sub >= SUBS // 2)

            @pl.when((h < NZ // 2 - 1) | mine)
            def _():
                p_copy(way, h, sub).wait_recv()

            @pl.when((h < NZ // 2 - 2) | ((h == NZ // 2 - 2) & mine))
            def _():
                p_copy(way, h + 1, sub).start()

    def c_event(i):
        for way in range(2):
            if way == 0:
                c_copy(way, i).wait_recv()

                @pl.when(i < NZ // 2 - 1)
                def _():
                    c_copy(way, i + 1).start()
            else:

                @pl.when(i < NZ // 2 - 1)
                def _():
                    c_copy(way, i).wait_recv()

                @pl.when(i < NZ // 2 - 2)
                def _():
                    c_copy(way, i + 1).start()

    def more_events(i, _):
        p_event(i)

        @pl.when((i % 2 == 1) & (i < 16))
        def _():
            c_event(i // 2)

        self_top(i // 8, (i % 8) * 8, 8)
        return 0

    lax.fori_loop(0, 8, more_events, 0)
    y_forward(vy_copy)
    lax.fori_loop(8, 16, more_events, 0)

    y_done(vy_copy)

    tab_copy.wait()
    for way in range(2):

        def pick_row(slot, _, way=way):
            j = tab_s[way, slot] & 31
            shift = (targets[j] - bulk) & 63
            to_z = (z + shift) & 15
            from_y = ((y * NZ + to_z - shift) & 63) >> 4
            for c in range(3):
                line = v_y[from_y * 3 + c, pl.ds(j, 1), :]
                for b in range(4):
                    row, col = divmod(c * 4 + b, 3)
                    v_rg[way * 9 * NB + slot, pl.ds(row, 1), pl.ds(col * 128, 128)] = line[
                        :, b * 128 : (b + 1) * 128
                    ]
            return 0

        lax.fori_loop(0, NB, pick_row, 0, unroll=4)
    for k in range(2):
        cy_copy(k).start()
    lax.fori_loop(16, 24, more_events, 0)

    y_forward(cy_copy)
    lax.fori_loop(24, 32, more_events, 0)

    own_p.wait()
    for d in range(1, NY):
        d_copy(d).wait_recv()
    codes_copy = pltpu.make_async_copy(codes_v, codes_s, loc.at[2])
    codes_copy.start()
    codes_copy.wait()

    for way in range(2):
        for sub in range(3):
            v_copy(way, 1, sub).start()

    def leaf_at(number):
        return p_all[(number >> 5) & 15, number & 31]

    for a in range(ACT):
        for d in range(1, NY):
            to_y = (y + d) % NY

            def fill(e, _, a=a, d=d, to_y=to_y):
                l_send[d - 1, a, e] = leaf_at(codes_s[to_y, a, e])
                return 0

            lax.fori_loop(0, LPER, fill, 0, unroll=True)
            l_copy(a, d).start()

        def fill_own(e, _, a=a):
            l_rec[a][y, e] = leaf_at(code_of(a, e))
            return 0

        lax.fori_loop(0, LPER, fill_own, 0, unroll=True)

    def pick_moved(j, _):
        from_z = (bulk - (targets[j] - bulk)) & 15
        p_rec[y * NB + j] = p_all[from_z, j]
        return 0

    lax.fori_loop(0, NB, pick_moved, 0, unroll=8)
    for k in range(2):
        pr_copy(k).start()

    y_done(cy_copy)

    def pick_cell(i, _):
        f = cell_lists[i // CPER, i % CPER]
        peer = f >> 4
        col = cell_req[f & 15, peer] & 255
        chosen[pl.ds(i, 1), :] = c_all[peer, pl.ds(col & 31, 1), :]
        picks[pl.ds(i, 1), :] = jnp.full((1, 128), col >> 5, jnp.int32)
        return 0

    lax.fori_loop(0, ACT * CPER, pick_cell, 0, unroll=8)
    got = chosen[...]
    group = picks[...]
    one = jnp.where(group == 0, got, 0.0)
    for g in range(1, 8):
        one = jnp.where(group == g, pltpu.roll(got, 128 - 16 * g, 1), one)
    near[...] = jnp.transpose(one)
    for a in range(ACT):
        near_part(a, 0, OCT)

    hops = [(h, sub) for h in range(1, 9) for sub in range(3) if V_CAP[h] > sub * 10]

    def v_event(i):
        h, sub = hops[i]
        for way in range(2):
            v_copy(way, h, sub).wait_recv()
            if (h + 1, sub) in hops:
                v_copy(way, h + 1, sub).start()

    def v_events(lo, hi):
        for i in range(lo, hi):
            v_event(i)

    for a in range(ACT):
        for d in range(1, NY):
            l_copy(a, d).wait_recv()
        if a == 3:
            y_forward(pr_copy)

        def block(e, _, a=a):
            from_y = (code_of(a, e) >> 9) & 3
            src = src_rows(lambda c, cut: l_rec[a][from_y, e, pl.ds(c, 1), cut])

            def step(i, _):
                at = pl.ds(pl.multiple_of(i * 8, 8), 8)
                px, py, pz = pts[a, 0, at, :], pts[a, 1, at, :], pts[a, 2, at, :]
                accs = tuple(acc[a, c, at, :] for c in range(3))
                accs = pair_terms(px, py, pz, src, accs)
                for c in range(3):
                    acc[a, c, at, :] = accs[c]
                return 0

            lax.fori_loop(0, OCT, step, 0, unroll=8)

            for at, number in V_PLAN[a]:

                @pl.when(e == at)
                def _(number=number):
                    v_event(number)

            if a >= 2:

                @pl.when(e == 3)
                def _():
                    k_close(a - 2)

            if a == 3:

                @pl.when(e == 2)
                def _():
                    y_send(0)

            return 0

        lax.fori_loop(0, LPER, block, 0)
        alive = jnp.where(a < act_cnt[0], step_time, 0.0)
        for c in range(3):
            pull = jnp.sum(jnp.transpose(acc[a, c]), axis=0, keepdims=True) * alive
            for b in range(4):
                row, col = divmod(c * 4 + b, 3)
                k_all[a][bulk, pl.ds(row, 1), pl.ds(col * 128, 128)] = pull[
                    :, b * 128 : (b + 1) * 128
                ]
        if a < ACT - 1:
            k_far(a)
        else:
            k_row(a)

    for d in range(1, NL):
        t_copy(d).wait_send()

    def p_sent(i, _):
        h = i // SUBS
        sub = i % SUBS
        for way in range(2):
            mine = (sub < SUBS // 2) if way == 0 else (sub >= SUBS // 2)

            @pl.when((h < NZ // 2 - 1) | mine)
            def _():
                p_copy(way, h, sub).wait_send()

        return 0

    lax.fori_loop(0, 32, p_sent, 0)
    y_send(1)
    k_close(2)
    v_events(16, 17)
    for h in range(NZ // 2):
        c_copy(0, h).wait_send()
        if h < NZ // 2 - 1:
            c_copy(1, h).wait_send()
    for k in range(4):
        vy_copy(k).wait_send()
        cy_copy(k).wait_send()
    for d in range(1, NY):
        d_copy(d).wait_send()
        for a in range(ACT):
            l_copy(a, d).wait_send()
    y_send(2)
    v_events(17, 18)
    y_done(pr_copy)
    for k in range(4):
        pr_copy(k).wait_send()
    y_send(3)
    v_events(18, 20)
    for h, sub in hops:
        for way in range(2):
            v_copy(way, h, sub).wait_send()
    for a in range(ACT):
        for dist in range(1, NZ):
            kz_copy(a, dist).wait_send()
    for a in range(ACT):
        for d in range(1, NY):
            ky_copy(a, d).wait_recv()

    def place(j, _):
        source = (bulk - (targets[j] - bulk)) & 63
        from_y = source >> 4
        spot_j = tab_s[2, j]
        number = j.astype(jnp.float32)
        hits = [c_all[source, pl.ds(32 + a, 1), :] == number for a in range(ACT)]
        for c in range(3):
            parts = []
            for b in range(4):
                row, col = divmod(c * 4 + b, 3)
                cut = pl.ds(col * 128, 128)
                kick = jnp.zeros((1, 128), jnp.float32)
                for a in range(ACT):
                    got = k_all[a][source, pl.ds(row, 1), cut]
                    kick = kick + jnp.where(hits[a], got, 0.0)
                parts.append(v_rg[spot_j, pl.ds(row, 1), cut] + kick)
            speed = jnp.concatenate(parts, axis=1)
            outv[c, pl.ds(j, 1), :] = speed
            outp[j, pl.ds(c, 1), :] = p_rec[from_y * NB + j, pl.ds(c, 1), :] + step_time * speed
        outp[j, pl.ds(3, 1), :] = p_rec[from_y * NB + j, pl.ds(3, 1), :]
        return 0

    lax.fori_loop(0, NB, place, 0, unroll=4)

    for a in range(ACT):
        for d in range(1, NY):
            ky_copy(a, d).wait_send()


def on_device(
    particles,
    velocities,
    cell_table,
    top_cells,
    active_ids,
    active_count,
    cell_requests,
    cell_lists,
    leaf_requests,
    leaf_lists,
    targets,
):
    speeds = jnp.transpose(velocities, (1, 0, 2))
    vmem = pl.BlockSpec(memory_space=pltpu.VMEM)
    smem = pl.BlockSpec(memory_space=pltpu.SMEM)
    f32 = jnp.float32
    dma = pltpu.SemaphoreType.DMA
    placed, moved = pl.pallas_call(
        kernel,
        out_shape=(
            jax.ShapeDtypeStruct((NB, 4, 512), f32),
            jax.ShapeDtypeStruct((3, NB, 512), f32),
        ),
        in_specs=[vmem] * 4 + [smem] * 7,
        out_specs=(vmem, vmem),
        scratch_shapes=[
            pltpu.VMEM((NZ, NB, 4, 512), f32),
            pltpu.VMEM((2 * 9 * NB, 4, 384), f32),
            pltpu.VMEM((8, 128), jnp.int32),
            pltpu.SMEM((8, 128), jnp.int32),
            pltpu.VMEM((NY * 3, NB, 512), f32),
            pltpu.VMEM((NY * NZ, 40, 128), f32),
            pltpu.VMEM((NL, 16, 128), f32),
            pltpu.VMEM((16, 512), f32),
            pltpu.VMEM((NY, 8, 128), jnp.int32),
            pltpu.SMEM((NY, 8, 128), jnp.int32),
            pltpu.VMEM((NY - 1, ACT, LPER, 4, 512), f32),
        ]
        + [pltpu.VMEM((NY, LPER, 4, 512), f32)] * ACT
        + [pltpu.VMEM((NY * NZ, 4, 384), f32)] * ACT
        + [
            pltpu.VMEM((NY * NB, 4, 512), f32),
            pltpu.VMEM((ACT, 3, 512, 128), f32),
            pltpu.VMEM((ACT, 3, 512, 128), f32),
            pltpu.VMEM((ACT, 8, 512), f32),
            pltpu.VMEM((ACT * CPER, 128), f32),
            pltpu.VMEM((ACT * CPER, 128), jnp.int32),
            pltpu.VMEM((128, ACT * CPER), f32),
            dma((2, 8, SUBS)),
            dma((2, 8, SUBS)),
            dma((2, 8)),
            dma((2, 8)),
            dma((2, 9, 3)),
            dma((2, 9, 3)),
            dma((NL,)),
            dma((NL,)),
            dma((NY,)),
            dma((NY,)),
            dma((NY,)),
            dma((NY,)),
            dma((NY,)),
            dma((NY,)),
            dma((ACT, NY)),
            dma((ACT, NY)),
            dma((NY,)),
            dma((NY,)),
            dma((ACT, NZ)),
            dma((ACT, NZ)),
            dma((ACT, NY)),
            dma((ACT, NY)),
            dma((5,)),
        ],
        compiler_params=pltpu.CompilerParams(
            collective_id=0, has_side_effects=True, vmem_limit_bytes=56 * 1024 * 1024
        ),
    )(
        particles,
        speeds,
        cell_table,
        top_cells,
        active_ids,
        active_count,
        cell_lists,
        cell_requests[0].T,
        leaf_requests[0].T,
        leaf_lists,
        targets,
    )
    return placed, jnp.transpose(moved, (1, 0, 2))


def solution(mesh):
    placed = (
        P(("leaf", "bulk"), None, None),
        P(("leaf", "bulk"), None, None),
        P(None, ("leaf", "bulk")),
        P(None, "leaf"),
        P(("leaf", "bulk")),
        P(("leaf", "bulk")),
        P(("leaf", "bulk"), None, None),
        P(("leaf", "bulk"), None),
        P(("leaf", "bulk"), None, None),
        P(("leaf", "bulk"), None),
        P(("leaf", "bulk")),
    )
    return jax.shard_map(
        on_device,
        mesh=mesh,
        in_specs=placed,
        out_specs=(P(("leaf", "bulk"), None, None), P(("leaf", "bulk"), None, None)),
        check_vma=False,
    )
```
